256 devices in a mesh: dp: 4 (over y), expert: 64 (over z, x, core).
Axes of the slice: x: 4, y: 4, z: 8, core: 2. Of those that a mesh axis runs over, the one named last changes fastest.
Arguments:
- tokens: bfloat16 [32768, 2048], P(('dp', 'expert')), may hold values from -6 to 6
- cotangent: bfloat16 [32768, 2048], P(('dp', 'expert')), may hold values from -6 to 6
- expert_ids: int32 [32768, 8], P(('dp', 'expert')), may hold values from 0 to 63, all different within a row; in each aligned block of 128 rows (0 to 127, 128 to 255, ...) at most 24 rows name the same one
- gate_probs: float32 [32768, 8], P(('dp', 'expert')), may hold values from 0.05 to 1
- up_weight: bfloat16 [64, 2048, 768], P('expert', None, 'dp'), may hold values from -0.125 to 0.125
- down_weight: float32 [64, 768, 2048], P('expert', 'dp'), may hold values from -28 to 28
- moment1: float32 [64, 768, 2048], P('expert', 'dp'), may hold values from -60 to 60
- moment2: float32 [64, 768, 2048], P('expert', 'dp'), may hold values from 0.05 to 5
- pair_match: int32 [64], replicated, may hold values from 0 to 63, as said below
Outputs:
- down_out: float32 [64, 768, 2048], P('expert', 'dp')
- moment1_out: float32 [64, 768, 2048], P('expert', 'dp')
- moment2_out: float32 [64, 768, 2048], P('expert', 'dp')
The draws below stay inside these ranges and needn't reach their ends.
Inputs may be any that keep to these rules, and one draw needn't show every extreme that they name: `expert_ids`: each row names 8 different experts. Within the rows of one device (aligned blocks of 128 rows) no expert is named by more than 24 rows, a bound that some block reaches. A perfect matching: pair_match[pair_match[i]] = i and pair_match[i] != i for every i.
All inputs are finite; a program needn't handle non-finite values.
Results may differ from the reference program's by a relative error of at most 0.00035.
Values may be sent and summed in bfloat16 or wider, within the bound.
A program may use at most 128 MiB of HBM per device.

```python
import math
import jax
import jax.numpy as jnp
import numpy as np
from jax import lax

D = 2048
FFN = 768
TOK_DEV = 128
EXPERTS = 64
TOP = 8
CAP = 24
TOKENS = 32768
N_DP = 4


def draw_pair_match(key, part):
    ordering = jax.random.permutation(key, EXPERTS).astype(jnp.int32)
    flipped = ordering.reshape(EXPERTS // 2, 2)[:, ::-1].reshape(EXPERTS)
    return jnp.zeros((EXPERTS,), jnp.int32).at[ordering].set(flipped)


def draw_down_weight(key, part):
    key_noise = jax.random.fold_in(key, 11)
    key_rows = jax.random.fold_in(key, 12)
    key_cols = jax.random.fold_in(key, 13)
    position = jnp.arange(FFN, dtype=jnp.float32) / FFN
    top_scale = 4.0
    noise = jnp.clip(jax.random.normal(key_noise, (EXPERTS, FFN, D), jnp.float32), -4.0, 4.0)
    row_scale = jnp.exp(jnp.log(top_scale) * position)
    row_factor = jax.random.uniform(key_rows, (EXPERTS, FFN, 1), jnp.float32, 0.7, 1.4)
    col_factor = jnp.exp(jax.random.uniform(key_cols, (EXPERTS, 1, D), jnp.float32, -0.6931, 0.6931))
    return 0.25 * noise * row_scale[None, :, None] * row_factor * col_factor


def shard_levels(rng, extent, pieces, smallest, high):
    gain = 1.0
    for dim, parts in pieces:
        steps = jax.random.uniform(jax.random.fold_in(jax.random.fold_in(rng, 6), dim), (parts,), jnp.float32, smallest / len(pieces), high / len(pieces))
        gain = gain * jnp.repeat(jnp.exp(steps), extent[dim] // parts).reshape((-1,) + (1,) * (len(extent) - 1 - dim))
    return gain


def deal_out(own_key, own, number, rows, amount, top, bound, lean):
    sequence = jax.random.permutation(own_key, amount)
    crowded, common = portions_of(amount, rows * top, bound, lean, True), portions_of(amount, rows * top, bound, lean, False)
    places = jnp.arange(amount)

    def named(sizes, rotation):
        used = int((sizes > 0).sum())
        fixed = max(1, used // 4)
        moved = fixed + (places - fixed + rotation * (used - fixed)) % max(1, amount - fixed)
        return jnp.zeros((amount,), jnp.int32).at[sequence[jnp.where(places < fixed, places, moved)]].set(jnp.asarray(sizes, jnp.int32))

    sizes = jnp.where(number % 4 == 0, named(crowded, number // 4), named(common, number - number // 4 - 1))
    mixed = jax.random.permutation(jax.random.fold_in(own, 3), amount)
    donor, taker = mixed[0:amount // 2 * 2:2], mixed[1:amount // 2 * 2:2]
    margin = jnp.minimum(sizes[donor] - 1, bound - sizes[taker]) // 2
    margin = jnp.where((donor == sequence[0]) | (taker == sequence[0]) | (sizes[taker] == 0), 0, jnp.maximum(margin, 0))
    moved = jax.random.randint(jax.random.fold_in(own, 4), (amount // 2,), 0, 1 << 20) % (margin + 1)
    sizes = sizes.at[donor].add(-moved).at[taker].add(moved)
    items = jnp.searchsorted(jnp.cumsum(sizes), jnp.arange(rows * top), side="right").astype(jnp.int32)
    listing = items.reshape(top, rows).T
    listing = listing[jax.random.permutation(jax.random.fold_in(own, 1), rows)]
    rotation = jax.random.randint(jax.random.fold_in(own, 2), (rows, 1), 0, top)
    return jnp.take_along_axis(listing, (jnp.arange(top)[None, :] + rotation) % top, axis=1)


def portions_of(number_of, total, reach, slope, full):
    portions = [(1 << 20) // math.isqrt(standing ** slope) + 1 for standing in range(1, number_of + 1)]
    largest = reach if full else min(reach, max(-(-total // number_of), total * portions[0] // sum(portions)))
    least = 1 if total - largest >= number_of - 1 else 0
    counts, rest = [largest] + [least] * (number_of - 1), total - largest - least * (number_of - 1)
    while rest > 0:
        candidates = [i for i in range(1, number_of) if counts[i] < largest] or [i for i in range(1, number_of) if counts[i] < reach]
        whole, left = sum([portions[i] for i in candidates]), rest
        for i in candidates:
            addition = min(reach - counts[i], max(1, left * portions[i] // whole), rest)
            counts[i] = counts[i] + addition
            rest = rest - addition
    return np.array(counts)


def bell_draw(stream_key, shape, scale, reach, pieces=(), held_as=jnp.bfloat16):
    result = scale * jax.random.normal(stream_key, shape, jnp.float32)
    if pieces:
        result = result * shard_levels(stream_key, shape, pieces, -0.22, 0.18)
    return jnp.clip(result, -reach, reach).astype(held_as)


def setup_inputs(seed: int = 0) -> dict:
    key_of = jax.random.split(jax.random.key(seed), 10)
    tokens = bell_draw(key_of[0], (TOKENS, D), 1.0, 6.0, ((0, 256),))
    cotangent = bell_draw(key_of[1], (TOKENS, D), 1.0, 6.0, ((0, 256),))
    expert_ids_keys = jax.random.split(jax.random.fold_in(key_of[2], 1), TOKENS // TOK_DEV)
    expert_ids_turns = jax.random.permutation(jax.random.fold_in(key_of[2], 3), TOKENS // TOK_DEV)
    expert_ids = jax.vmap(lambda own, number: deal_out(jax.random.fold_in(key_of[2], 2), own, number, TOK_DEV, EXPERTS, TOP, CAP, 2))(expert_ids_keys, expert_ids_turns).reshape((TOKENS, TOP))
    gate_probs = jnp.clip(jnp.exp(math.log(1.0) - 2.9957323 * jax.random.uniform(key_of[3], (TOKENS, TOP), jnp.float32) ** shard_levels(key_of[3], (TOKENS, TOP), ((0, 256),), -0.2, 0.2)), 0.05, 1.0)
    up_weight = bell_draw(key_of[4], (EXPERTS, D, FFN), D ** -0.5, 0.125, ((0, 64), (2, 4)))
    down_weight = draw_down_weight(jax.random.fold_in(key_of[9], 71), 0)
    moment1 = bell_draw(key_of[6], (EXPERTS, FFN, D), 10.0, 60.0, ((0, 64), (1, 4)), jnp.float32)
    moment2 = jnp.clip(jnp.exp(math.log(5.0) - 4.6051702 * jax.random.uniform(key_of[7], (EXPERTS, FFN, D), jnp.float32) ** shard_levels(key_of[7], (EXPERTS, FFN, D), ((0, 64), (1, 4)), -0.2, 0.2)), 0.05, 5.0)
    pair_match = draw_pair_match(jax.random.fold_in(key_of[9], 71), 0)
    return dict(tokens=tokens, cotangent=cotangent, expert_ids=expert_ids, gate_probs=gate_probs, up_weight=up_weight, down_weight=down_weight, moment1=moment1, moment2=moment2, pair_match=pair_match)


beta_one = 0.9
beta_two = 0.999
epsilon = 1e-06
learn_rate = 0.05

def reference(tokens, cotangent, expert_ids, gate_probs, up_weight, down_weight, moment1, moment2, pair_match):
    most_rows = N_DP * EXPERTS * CAP
    flat_ids = expert_ids.reshape(-1)
    flat_probs = gate_probs.reshape(-1)
    flat_rows = (jnp.arange(TOKENS * TOP, dtype=jnp.int32) // TOP).astype(jnp.int32)

    def one_expert(expert):
        matched = flat_ids == expert
        ordering = jnp.argsort(jnp.where(matched, 0, 1).astype(jnp.int32), stable=True)[:most_rows].astype(jnp.int32)
        chosen = matched[ordering]
        row_index = flat_rows[ordering]
        gathered = tokens[row_index]
        weights_row = jnp.where(chosen, flat_probs[ordering], jnp.float32(0.0))
        scaled = (weights_row[:, None] * cotangent[row_index].astype(jnp.float32)).astype(jnp.bfloat16)
        pre_act = jnp.dot(gathered, up_weight[expert], preferred_element_type=jnp.float32)
        hidden = jax.nn.silu(pre_act).astype(jnp.bfloat16)
        return jnp.dot(hidden.T, scaled, preferred_element_type=jnp.float32)
    gradient = lax.map(one_expert, jnp.arange(EXPERTS, dtype=jnp.int32))
    first = beta_one * moment1 + (1.0 - beta_one) * gradient
    second = beta_two * moment2 + (1.0 - beta_two) * gradient * gradient
    update = first / (jnp.sqrt(second) + epsilon)
    weight_norm = jnp.sqrt(lax.optimization_barrier(jnp.sum(down_weight * down_weight, axis=(1, 2))))
    update_norm = jnp.sqrt(lax.optimization_barrier(jnp.sum(update * update, axis=(1, 2))))
    trust = weight_norm / (update_norm + epsilon)
    renewed = down_weight - learn_rate * trust[:, None, None] * update
    return (renewed[pair_match], first[pair_match], second[pair_match])
```

```python
import functools

import jax
import jax.numpy as jnp
from jax import lax
from jax.experimental import pallas as pl
from jax.experimental.pallas import tpu as pltpu
from jax.sharding import PartitionSpec as P

beta_one = 0.9
beta_two = 0.999
epsilon = 1e-06
learn_rate = 0.05

NZ = 8
PLANE = 8
NY = 4
CAP = 24
TOK = 128
PAIRS = NZ // 2
CHUNKS = 4
MESH = pl.DeviceIdType.MESH


def gradient_kernel(
    tok, cot, meta, up, out,
    zt, zc, zm, sel, prob, sbt, sbs, rbt, rbs, upb, hid, gbuf, grecv,
    zt_s, zt_r, zm_s, zm_r, zc_s, zc_r, up_s, up_r, xt_s, xt_r, xc_s, xc_r, g_s, g_r, loc,
):
    f32, bf16 = jnp.float32, jnp.bfloat16
    width = tok.shape[1]
    chunk = width // CHUNKS
    slice_rows = up.shape[0]
    y = lax.axis_index("dp")
    e = lax.axis_index("expert")
    total = NZ * PLANE
    z = e // PLANE
    p = lax.rem(e, PLANE)
    right = (y, lax.rem(e + PLANE, total))
    left = (y, lax.rem(e + total - PLANE, total))

    def mate(o):
        q = lax.rem(p + o, PLANE)
        return q, (y, z * PLANE + q)

    def layer(o):
        k = lax.rem(y + o, NY)
        return k, (k, e)

    barrier = pltpu.get_barrier_semaphore()
    partners = [right, left]
    partners += [mate(o)[1] for o in range(1, PLANE)]
    partners += [layer(o)[1] for o in range(1, NY)]
    for partner in partners:
        pl.semaphore_signal(barrier, inc=1, device_id=partner, device_id_type=MESH)
    pl.semaphore_wait(barrier, len(partners))

    def remote(src, dst, send, recv, device):
        return pltpu.make_async_remote_copy(
            src_ref=src, dst_ref=dst, send_sem=send, recv_sem=recv,
            device_id=device, device_id_type=MESH,
        )

    def held(direction, step):
        return 0 if step == 1 else 2 * (step - 1) + direction

    def landing(direction, step):
        return 1 if step == 4 else 2 * step + direction

    half = TOK // 2

    def z_copy(ring, send, recv, direction, step):
        src, dst = ring.at[held(direction, step)], ring.at[landing(direction, step)]
        if step == 4:
            rows = pl.ds(direction * half, half)
            src, dst = src.at[rows], dst.at[rows]
        return remote(src, dst, send.at[direction, step], recv.at[direction, step],
                      left if direction else right)

    def tok_copy(direction, step):
        return z_copy(zt, zt_s, zt_r, direction, step)

    def cot_copy(c, direction, step):
        return z_copy(zc.at[c], zc_s.at[c], zc_r.at[c], direction, step)

    def meta_copy(direction, step):
        return remote(zm.at[held(direction, step)], zm.at[landing(direction, step)],
                      zm_s.at[direction, step], zm_r.at[direction, step],
                      left if direction else right)

    def meta_steps(step):
        return (0,) if step == 4 else (0, 1)

    zm[0] = meta[...]
    zt[0] = tok[...]
    for c in range(CHUNKS):
        zc[c, 0] = cot[:, c * chunk:(c + 1) * chunk]

    for d in (0, 1):
        meta_copy(d, 1).start()
        tok_copy(d, 1).start()

    own_up = pltpu.make_async_copy(up, upb.at[y], loc.at[0])
    own_up.start()

    def up_copy(o):
        k, device = layer(o)
        return remote(up, upb.at[y], up_s.at[o], up_r.at[o], device)

    for o in (2, 1, 3):
        up_copy(o).start()

    for c in range(CHUNKS):
        for d in (0, 1):
            cot_copy(c, d, 1).start()

    row_of = lax.broadcasted_iota(jnp.int32, (TOK, TOK), 0)
    col_of = lax.broadcasted_iota(jnp.int32, (TOK, TOK), 1)
    before = (row_of < col_of).astype(f32).astype(bf16)
    first_expert = (z * PLANE).astype(f32)
    expert_of = lax.broadcasted_iota(jnp.int32, (PLANE, TOK), 0).astype(f32) + first_expert
    place_of = lax.broadcasted_iota(jnp.int32, (PLANE, CAP, TOK), 1).astype(f32)

    def select_of(slot):
        mask = jnp.zeros((PLANE, TOK), f32)
        weight = jnp.zeros((PLANE, TOK), f32)
        top = meta.shape[0] // 2
        for k in range(top):
            hit = zm[slot, k:k + 1, :] == expert_of
            mask = jnp.where(hit, 1.0, mask)
            weight = jnp.where(hit, zm[slot, top + k:top + k + 1, :], weight)
        rank = jnp.dot(mask.astype(bf16), before, preferred_element_type=f32)
        rank = jnp.where(mask > 0.5, rank, -1.0)
        picked = jnp.where(rank[:, None, :] == place_of, 1.0, 0.0)
        gate = jnp.sum(picked * weight[:, None, :], axis=2, keepdims=True)
        return picked, gate

    def build(j):
        first_pick, first_gate = select_of(2 * j)
        second_pick, second_gate = select_of(2 * j + 1)
        blank = jnp.zeros((PLANE, CAP, TOK), f32)
        both = jnp.concatenate(
            [jnp.concatenate([first_pick, blank], axis=2),
             jnp.concatenate([blank, second_pick], axis=2)], axis=1)
        sel[j] = both.reshape(PLANE * 2 * CAP, 2 * TOK).astype(bf16)
        prob[j] = jnp.concatenate([first_gate, second_gate], axis=1).reshape(PLANE * 2 * CAP, 1)

    def xt_copy(j, o):
        q, device = mate(o)
        return remote(sbt.at[j, q], rbt.at[p, j], xt_s.at[j, o], xt_r.at[j, o], device)

    def xt_own(j):
        return pltpu.make_async_copy(sbt.at[j, p], rbt.at[p, j], loc.at[1 + j])

    def xc_copy(c, o):
        q, device = mate(o)
        return remote(sbs.at[c, q], rbs.at[c, p], xc_s.at[c, o], xc_r.at[c, o], device)

    def xc_own(c):
        return pltpu.make_async_copy(sbs.at[c, p], rbs.at[c, p], loc.at[1 + PAIRS + c])

    order = (4, 2, 6, 3, 5, 1, 7)

    def send_tokens(j):
        build(j)

        @pl.loop(0, CHUNKS)
        def _(c):
            cols = pl.ds(pl.multiple_of(c * chunk, chunk), chunk)
            pair = zt[2 * j:2 * j + 2, :, cols].reshape(2 * TOK, chunk)
            rows = jnp.dot(sel[j], pair, preferred_element_type=f32)
            sbt[j, :, :, cols] = rows.astype(bf16).reshape(PLANE, 2 * CAP, chunk)

        xt_own(j).start()
        for o in order:
            xt_copy(j, o).start()

    for step in (1, 2, 3, 4):
        for d in (0, 1):
            if d in meta_steps(step):
                meta_copy(d, step).wait_recv()
                if step < 4 and d in meta_steps(step + 1):
                    meta_copy(d, step + 1).start()
            tok_copy(d, step).wait_recv()
            if step < 4:
                tok_copy(d, step + 1).start()
        send_tokens(0 if step == 4 else step)

    for step in (1, 2, 3, 4):
        for c in range(CHUNKS):
            for d in (0, 1):
                cot_copy(c, d, step).wait_recv()
                if step < 4:
                    cot_copy(c, d, step + 1).start()
            if step == 4:
                for j in range(PAIRS):
                    pair = zc[c, 2 * j:2 * j + 2].reshape(2 * TOK, chunk)
                    rows = jnp.dot(sel[j], pair, preferred_element_type=f32) * prob[j]
                    sbs[c, :, j] = rows.astype(bf16).reshape(PLANE, 2 * CAP, chunk)
                xc_own(c).start()
                for o in order:
                    xc_copy(c, o).start()

    own_up.wait()
    for o in range(1, NY):
        up_copy(o).wait_recv()
    for j in range(PAIRS):
        xt_own(j).wait()
        for o in range(1, PLANE):
            xt_copy(j, o).wait_recv()
    span = 2 * PAIRS * 2 * CAP

    @pl.loop(0, PLANE // 2)
    def _(m):
        rows = rbt[pl.ds(2 * m, 2)].reshape(span, width)
        cols = pl.ds(pl.multiple_of(m * span, span), span)

        @pl.loop(0, NY)
        def _(k):
            v = lax.dot_general(upb[k], rows, (((1,), (1,)), ((), ())), preferred_element_type=f32)
            units = pl.ds(pl.multiple_of(k * slice_rows, slice_rows), slice_rows)
            hid[units, cols] = (v / (1.0 + jnp.exp(-v))).astype(bf16)

    def g_copy(c, o):
        k, device = layer(o)
        return remote(gbuf.at[c, k], grecv.at[c, o - 1], g_s.at[c, o], g_r.at[c, o], device)

    for c in range(CHUNKS):
        xc_own(c).wait()
        for o in range(1, PLANE):
            xc_copy(c, o).wait_recv()

        @pl.loop(0, NY)
        def _(k):
            units = pl.ds(pl.multiple_of(k * slice_rows, slice_rows), slice_rows)
            rows = rbs[c].reshape(PLANE * PAIRS * 2 * CAP, chunk)
            gbuf[c, k] = jnp.dot(hid[units, :], rows, preferred_element_type=f32)

        for o in (2, 1, 3):
            g_copy(c, o).start()

    for c in range(CHUNKS):
        for o in range(1, NY):
            g_copy(c, o).wait_recv()
        summed = (gbuf[c, y] + grecv[c, 0]) + (grecv[c, 1] + grecv[c, 2])
        out[:, c * chunk:(c + 1) * chunk] = summed

    for step in (1, 2, 3, 4):
        for d in (0, 1):
            if d in meta_steps(step):
                meta_copy(d, step).wait_send()
            tok_copy(d, step).wait_send()
            for c in range(CHUNKS):
                cot_copy(c, d, step).wait_send()
    for o in range(1, NY):
        up_copy(o).wait_send()
        for c in range(CHUNKS):
            g_copy(c, o).wait_send()
    for o in range(1, PLANE):
        for j in range(PAIRS):
            xt_copy(j, o).wait_send()
        for c in range(CHUNKS):
            xc_copy(c, o).wait_send()


def expert_gradient(tokens, cotangent, expert_ids, gate_probs, up_weight):
    rows, width = tokens.shape
    chunk = width // CHUNKS
    units = up_weight.shape[2]
    bf16, f32 = jnp.bfloat16, jnp.float32
    meta = jnp.concatenate([expert_ids.astype(f32).T, gate_probs.T], axis=0)
    up = up_weight[0].T
    pick = PLANE * 2 * CAP
    dma = pltpu.SemaphoreType.DMA
    return pl.pallas_call(
        gradient_kernel,
        out_shape=jax.ShapeDtypeStruct((units, width), f32),
        in_specs=[pl.BlockSpec(memory_space=pltpu.VMEM)] * 4,
        out_specs=pl.BlockSpec(memory_space=pltpu.VMEM),
        scratch_shapes=[
            pltpu.VMEM((NZ, rows, width), bf16),
            pltpu.VMEM((CHUNKS, NZ, rows, chunk), bf16),
            pltpu.VMEM((NZ,) + meta.shape, f32),
            pltpu.VMEM((PAIRS, pick, 2 * rows), bf16),
            pltpu.VMEM((PAIRS, pick, 1), f32),
            pltpu.VMEM((PAIRS, PLANE, 2 * CAP, width), bf16),
            pltpu.VMEM((CHUNKS, PLANE, PAIRS, 2 * CAP, chunk), bf16),
            pltpu.VMEM((PLANE, PAIRS, 2 * CAP, width), bf16),
            pltpu.VMEM((CHUNKS, PLANE, PAIRS, 2 * CAP, chunk), bf16),
            pltpu.VMEM((NY, units, width), bf16),
            pltpu.VMEM((NY * units, PAIRS * pick), bf16),
            pltpu.VMEM((CHUNKS, NY, units, chunk), f32),
            pltpu.VMEM((CHUNKS, NY - 1, units, chunk), f32),
            dma((2, 5)), dma((2, 5)),
            dma((2, 5)), dma((2, 5)),
            dma((CHUNKS, 2, 5)), dma((CHUNKS, 2, 5)),
            dma((NY,)), dma((NY,)),
            dma((PAIRS, PLANE)), dma((PAIRS, PLANE)),
            dma((CHUNKS, PLANE)), dma((CHUNKS, PLANE)),
            dma((CHUNKS, NY)), dma((CHUNKS, NY)),
            dma((1 + PAIRS + CHUNKS,)),
        ],
        compiler_params=pltpu.CompilerParams(
            collective_id=0, has_side_effects=True, vmem_limit_bytes=62 * 2**20
        ),
        cost_estimate=pl.CostEstimate(
            flops=4 * PAIRS * pick * width * units * NY,
            bytes_accessed=4 * rows * width + 2 * units * width * 3,
            transcendentals=PAIRS * pick * units * NY,
        ),
    )(tokens, cotangent, meta, up)


def pick_kernel(match, src, out):
    @pl.loop(0, src.shape[0])
    def _(i):
        out[i] = src[match[i]]


def relocate(states, pair_match):
    group_size = lax.axis_size("expert")
    count = len(states)
    rows, width = states[0].shape
    high, lanes = rows // 4, 128
    across = width // lanes
    pieces = [s.reshape(4, high, across, lanes).transpose(0, 2, 1, 3) for s in states]
    stacked = jnp.stack(pieces, axis=2).reshape(group_size, count * high, lanes)
    spread = lax.all_to_all(stacked, "expert", split_axis=0, concat_axis=0, tiled=True)
    chosen = pl.pallas_call(
        pick_kernel,
        out_shape=jax.ShapeDtypeStruct(spread.shape, spread.dtype),
        in_specs=[pl.BlockSpec(memory_space=pltpu.SMEM), pl.BlockSpec(memory_space=pltpu.VMEM)],
        out_specs=pl.BlockSpec(memory_space=pltpu.VMEM),
        compiler_params=pltpu.CompilerParams(vmem_limit_bytes=32 * 2**20),
    )(pair_match, spread)
    arrived = lax.all_to_all(chosen, "expert", split_axis=0, concat_axis=0, tiled=True)
    arrived = arrived.reshape(4, across, count, high, lanes).transpose(2, 0, 3, 1, 4)
    arrived = arrived.reshape(count, rows, width)
    return tuple(arrived[i] for i in range(count))


def lamb_step(weight, moment_one, moment_two, gradient):
    first = beta_one * moment_one + (1.0 - beta_one) * gradient
    second = beta_two * moment_two + (1.0 - beta_two) * gradient * gradient
    update = first / (jnp.sqrt(second) + epsilon)
    weight_sq, update_sq = lax.psum((jnp.sum(weight * weight), jnp.sum(update * update)), "dp")
    trust_ratio = jnp.sqrt(weight_sq) / (jnp.sqrt(update_sq) + epsilon)
    renewed = weight - learn_rate * trust_ratio * update
    return (renewed, first, second)


def local(
    tokens, cotangent, expert_ids, gate_probs, up_weight, down_weight, moment1, moment2, pair_match
):
    gradient = expert_gradient(tokens, cotangent, expert_ids, gate_probs, up_weight)
    renewed, first, second = lamb_step(down_weight[0], moment1[0], moment2[0], gradient)
    renewed, first, second = relocate((renewed, first, second), pair_match)
    return (renewed[None], first[None], second[None])


def solution(mesh):
    in_specs = (
        P(("dp", "expert"), None),
        P(("dp", "expert"), None),
        P(("dp", "expert"), None),
        P(("dp", "expert"), None),
        P("expert", None, "dp"),
        P("expert", "dp", None),
        P("expert", "dp", None),
        P("expert", "dp", None),
        P(),
    )
    out_specs = (P("expert", "dp", None), P("expert", "dp", None), P("expert", "dp", None))
    return jax.shard_map(local, mesh=mesh, in_specs=in_specs, out_specs=out_specs, check_vma=False)
```

```python
import jax
import jax.numpy as jnp
from jax import lax
from jax.experimental import pallas as pl
from jax.experimental.pallas import tpu as pltpu
from jax.sharding import PartitionSpec as P

beta_one = 0.9
beta_two = 0.999
epsilon = 1e-06
learn_rate = 0.05

NZ = 8
PLANE = 8
NY = 4
CAP = 24
TOK = 128
PAIRS = NZ // 2
CHUNKS = 4
VMEM_BYTES = 62 * 2**20
TOTAL = NZ * PLANE
HIGH, LANES = 48, 128
ACROSS = 16
WORDS = HIGH // 2
STATES = 3
STEP = 0.6931471805599453 / 8.0
LEVELS = 32767.0
MESH = pl.DeviceIdType.MESH


def step_kernel(
    match, meta, tok, cot, up, weight, moment1, moment2, new_w, new_1, new_2,
    zt, zc, zm, sel, prob, sbt, sbs, rbt, rbs, upb, hid, gbuf, grecv,
    stg, mid, fin, upmid, upout, norm, norm_in,
    zt_s, zt_r, zm_s, zm_r, zc_s, zc_r, up_s, up_r, xt_s, xt_r, xc_s, xc_r, g_s, g_r, n_s, n_r,
    ex_s, ex_r, loc, load, store,
):
    f32, bf16, i32 = jnp.float32, jnp.bfloat16, jnp.int32
    width = tok.shape[1]
    chunk = width // CHUNKS
    per_chunk = chunk // LANES
    slice_rows = up.shape[0]
    groups = slice_rows // HIGH
    y = lax.axis_index("dp")
    e = lax.axis_index("expert")
    z = e // PLANE
    p = lax.rem(e, PLANE)
    right = (y, lax.rem(e + PLANE, TOTAL))
    left = (y, lax.rem(e + TOTAL - PLANE, TOTAL))

    def mate(o):
        q = lax.rem(p + o, PLANE)
        return q, (y, z * PLANE + q)

    def layer(o):
        k = lax.rem(y + o, NY)
        return k, (k, e)

    tok_load = pltpu.make_async_copy(tok, zt.at[0], load.at[0])
    tok_load.start()
    cot_loads = [
        pltpu.make_async_copy(cot.at[:, pl.ds(c * chunk, chunk)], zc.at[c, 0], load.at[1 + c])
        for c in range(CHUNKS)
    ]
    state_loads = [
        pltpu.make_async_copy(
            ref.at[:, pl.ds(c * chunk, chunk)], gbuf.at[a, c], load.at[1 + CHUNKS + a * CHUNKS + c])
        for a, ref in enumerate((weight, moment1, moment2)) for c in range(CHUNKS)
    ]
    for copy in state_loads + cot_loads:
        copy.start()
    zm[0] = meta[...]

    barrier = pltpu.get_barrier_semaphore()

    @pl.loop(1, TOTAL)
    def _(o):
        pl.semaphore_signal(
            barrier, inc=1, device_id=(y, lax.rem(e + o, TOTAL)), device_id_type=MESH)

    for o in range(1, NY):
        pl.semaphore_signal(barrier, inc=1, device_id=layer(o)[1], device_id_type=MESH)
    pl.semaphore_wait(barrier, TOTAL - 1 + NY - 1)

    def remote(src, dst, send, recv, device):
        return pltpu.make_async_remote_copy(
            src_ref=src, dst_ref=dst, send_sem=send, recv_sem=recv,
            device_id=device, device_id_type=MESH,
        )

    def held(direction, step):
        return 0 if step == 1 else 2 * (step - 1) + direction

    def landing(direction, step):
        return 1 if step == 4 else 2 * step + direction

    half = TOK // 2

    def z_copy(ring, send, recv, direction, step):
        src, dst = ring.at[held(direction, step)], ring.at[landing(direction, step)]
        if step == 4:
            rows = pl.ds(direction * half, half)
            src, dst = src.at[rows], dst.at[rows]
        return remote(src, dst, send.at[direction, step], recv.at[direction, step],
                      left if direction else right)

    def tok_copy(direction, step):
        return z_copy(zt, zt_s, zt_r, direction, step)

    def cot_copy(c, direction, step):
        return z_copy(zc.at[c], zc_s.at[c], zc_r.at[c], direction, step)

    def meta_copy(direction, step):
        return remote(zm.at[held(direction, step)], zm.at[landing(direction, step)],
                      zm_s.at[direction, step], zm_r.at[direction, step],
                      left if direction else right)

    def meta_steps(step):
        return (0,) if step == 4 else (0, 1)

    tok_load.wait()
    for d in (0, 1):
        meta_copy(d, 1).start()
        tok_copy(d, 1).start()

    def piece_of(q):
        rows = pl.ds(pl.multiple_of((q // ACROSS) * HIGH, HIGH), HIGH)
        cols = pl.ds(pl.multiple_of(lax.rem(q, ACROSS) * LANES, LANES), LANES)
        return rows, cols

    def all_pieces(buffer, index):
        span = pl.ds(0, TOTAL - 1)
        return remote(buffer.at[span], buffer.at[span], ex_s.at[index], ex_r.at[index], right)

    @pl.loop(1, TOTAL)
    def _(o):
        q = lax.rem(e + o, TOTAL)
        rows, cols = piece_of(q)
        remote(up.at[rows, cols], upmid.at[e], ex_s.at[0], ex_r.at[0], (y, q)).start()

    own_rows, own_cols = piece_of(e)
    own_up = pltpu.make_async_copy(up.at[own_rows, own_cols], upmid.at[e], loc.at[0])
    own_up.start()

    scale_row = lax.broadcasted_iota(i32, (8, LANES), 0)
    for copy in state_loads:
        copy.wait()

    @pl.loop(0, CHUNKS)
    def _(c):
        for h in range(per_chunk):
            for g in range(groups):
                q = g * ACROSS + c * per_chunk + h
                powers = jnp.zeros((8, LANES), f32)
                for a in range(STATES):
                    x = gbuf[a, c, g * HIGH:(g + 1) * HIGH, h * LANES:(h + 1) * LANES]
                    most = jnp.maximum(jnp.max(jnp.abs(x), axis=0, keepdims=True), 1e-30)
                    power = jnp.ceil(jnp.log(most) * (1.0 / STEP))
                    inverse = 1.0 / (jnp.exp(power * STEP) * (1.0 / LEVELS))
                    code = jnp.clip(jnp.floor(x * inverse + 0.5), -LEVELS, LEVELS).astype(i32)
                    stg[q, a * WORDS:(a + 1) * WORDS] = code[:WORDS] * 65536 + (code[WORDS:] + 32768)
                    powers = jnp.where(scale_row == a, power, powers)
                stg[q, STATES * WORDS:] = powers.astype(i32)

    @pl.loop(1, TOTAL)
    def _(o):
        q = lax.rem(e + o, TOTAL)
        remote(stg.at[q], mid.at[e], ex_s.at[1], ex_r.at[1], (y, q)).start()

    mid[e] = stg[e]

    def up_copy(o):
        k, device = layer(o)
        return remote(upb.at[y], upb.at[y], up_s.at[o], up_r.at[o], device)

    row_of = lax.broadcasted_iota(i32, (TOK, TOK), 0)
    col_of = lax.broadcasted_iota(i32, (TOK, TOK), 1)
    before = (row_of < col_of).astype(f32).astype(bf16)
    place_of = lax.broadcasted_iota(i32, (PLANE, CAP, TOK), 1).astype(f32)
    which = lax.broadcasted_iota(i32, (PLANE, TOK), 0)
    expert_of = jnp.zeros((PLANE, TOK), i32)
    for k in range(PLANE):
        expert_of = jnp.where(which == k, match[z * PLANE + k], expert_of)
    expert_of = expert_of.astype(f32)

    def select_of(slot):
        mask = jnp.zeros((PLANE, TOK), f32)
        gates = jnp.zeros((PLANE, TOK), f32)
        top = meta.shape[0] // 2
        for k in range(top):
            hit = zm[slot, k:k + 1, :] == expert_of
            mask = jnp.where(hit, 1.0, mask)
            gates = jnp.where(hit, zm[slot, top + k:top + k + 1, :], gates)
        rank = jnp.dot(mask.astype(bf16), before, preferred_element_type=f32)
        rank = jnp.where(mask > 0.5, rank, -1.0)
        picked = jnp.where(rank[:, None, :] == place_of, 1.0, 0.0)
        gate = jnp.sum(picked * gates[:, None, :], axis=2, keepdims=True)
        return picked, gate

    def build(j):
        first_pick, first_gate = select_of(2 * j)
        second_pick, second_gate = select_of(2 * j + 1)
        blank = jnp.zeros((PLANE, CAP, TOK), f32)
        both = jnp.concatenate(
            [jnp.concatenate([first_pick, blank], axis=2),
             jnp.concatenate([blank, second_pick], axis=2)], axis=1)
        sel[j] = both.reshape(PLANE * 2 * CAP, 2 * TOK).astype(bf16)
        prob[j] = jnp.concatenate([first_gate, second_gate], axis=1).reshape(PLANE * 2 * CAP, 1)

    def xt_copy(j, o):
        q, device = mate(o)
        return remote(sbt.at[j, q], rbt.at[p, j], xt_s.at[j, o], xt_r.at[j, o], device)

    def xt_own(j):
        return pltpu.make_async_copy(sbt.at[j, p], rbt.at[p, j], loc.at[1 + j])

    def xc_copy(c, o):
        q, device = mate(o)
        return remote(sbs.at[c, q], rbs.at[c, p], xc_s.at[c, o], xc_r.at[c, o], device)

    def xc_own(c):
        return pltpu.make_async_copy(sbs.at[c, p], rbs.at[c, p], loc.at[1 + PAIRS + c])

    order = (4, 2, 6, 3, 5, 1, 7)

    def send_tokens(j):
        build(j)

        @pl.loop(0, CHUNKS)
        def _(c):
            cols = pl.ds(pl.multiple_of(c * chunk, chunk), chunk)
            pair = zt[2 * j:2 * j + 2, :, cols].reshape(2 * TOK, chunk)
            rows = jnp.dot(sel[j], pair, preferred_element_type=f32)
            sbt[j, :, :, cols] = rows.astype(bf16).reshape(PLANE, 2 * CAP, chunk)

        xt_own(j).start()
        for o in order:
            xt_copy(j, o).start()

    landed = upb.at[y, own_rows, own_cols]
    last_up = pltpu.make_async_copy(upout.at[e], landed, loc.at[1 + PAIRS + CHUNKS])

    for step in (1, 2, 3, 4):
        for d in (0, 1):
            if d in meta_steps(step):
                meta_copy(d, step).wait_recv()
                if step < 4 and d in meta_steps(step + 1):
                    meta_copy(d, step + 1).start()
            tok_copy(d, step).wait_recv()
            if step < 4:
                tok_copy(d, step + 1).start()
        send_tokens(0 if step == 4 else step)
        if step == 2:
            own_up.wait()
            all_pieces(upmid, 0).wait_recv()

            @pl.loop(0, TOTAL)
            def _(i):
                upout[i] = upmid[match[i]]

            @pl.loop(1, TOTAL)
            def _(o):
                q = lax.rem(e + o, TOTAL)
                remote(upout.at[q], landed, ex_s.at[2], ex_r.at[2], (y, q)).start()

            last_up.start()
            for c in range(CHUNKS):
                cot_loads[c].wait()
                for d in (0, 1):
                    cot_copy(c, d, 1).start()

    last_up.wait()
    all_pieces(upout, 2).wait_recv()
    for o in (2, 1, 3):
        up_copy(o).start()

    all_pieces(stg, 1).wait_send()
    all_pieces(mid, 1).wait_recv()

    @pl.loop(0, TOTAL)
    def _(i):
        stg[i] = mid[match[i]]

    @pl.loop(1, TOTAL)
    def _(o):
        q = lax.rem(e + o, TOTAL)
        remote(stg.at[q], fin.at[e], ex_s.at[3], ex_r.at[3], (y, q)).start()

    fin[e] = stg[e]

    for step in (1, 2, 3, 4):
        for c in range(CHUNKS):
            for d in (0, 1):
                cot_copy(c, d, step).wait_recv()
                if step < 4:
                    cot_copy(c, d, step + 1).start()
            if step == 4:
                for j in range(PAIRS):
                    pair = zc[c, 2 * j:2 * j + 2].reshape(2 * TOK, chunk)
                    rows = jnp.dot(sel[j], pair, preferred_element_type=f32) * prob[j]
                    sbs[c, :, j] = rows.astype(bf16).reshape(PLANE, 2 * CAP, chunk)
                xc_own(c).start()
                for o in order:
                    xc_copy(c, o).start()

    for o in range(1, NY):
        up_copy(o).wait_recv()
    for j in range(PAIRS):
        xt_own(j).wait()
        for o in range(1, PLANE):
            xt_copy(j, o).wait_recv()
    span = 2 * PAIRS * 2 * CAP

    @pl.loop(0, PLANE // 2)
    def _(m):
        rows = rbt[pl.ds(2 * m, 2)].reshape(span, width)
        cols = pl.ds(pl.multiple_of(m * span, span), span)

        @pl.loop(0, NY)
        def _(k):
            v = lax.dot_general(upb[k], rows, (((1,), (1,)), ((), ())), preferred_element_type=f32)
            units = pl.ds(pl.multiple_of(k * slice_rows, slice_rows), slice_rows)
            hid[units, cols] = (v / (1.0 + jnp.exp(-v))).astype(bf16)

    def g_copy(c, o):
        k, device = layer(o)
        return remote(gbuf.at[c, k], grecv.at[c, o - 1], g_s.at[c, o], g_r.at[c, o], device)

    for c in range(CHUNKS):
        xc_own(c).wait()
        for o in range(1, PLANE):
            xc_copy(c, o).wait_recv()

        @pl.loop(0, NY)
        def _(k):
            units = pl.ds(pl.multiple_of(k * slice_rows, slice_rows), slice_rows)
            rows = rbs[c].reshape(PLANE * PAIRS * 2 * CAP, chunk)
            gbuf[c, k] = jnp.dot(hid[units, :], rows, preferred_element_type=f32)

        for o in (2, 1, 3):
            g_copy(c, o).start()

    all_pieces(fin, 3).wait_recv()
    norm[...] = jnp.zeros_like(norm)

    def put(ref, c, slot):
        return pltpu.make_async_copy(
            gbuf.at[c, slot], ref.at[:, pl.ds(c * chunk, chunk)], store.at[c, slot])

    for c in range(CHUNKS):
        for o in range(1, NY):
            g_copy(c, o).wait()

        @pl.loop(0, groups)
        def _(g):
            rows = pl.ds(pl.multiple_of(g * HIGH, HIGH), HIGH)
            for h in range(per_chunk):
                q = g * ACROSS + c * per_chunk + h
                cols = slice(h * LANES, (h + 1) * LANES)
                powers = fin[q, STATES * WORDS:].astype(f32)
                scales = jnp.exp(powers * STEP) * (1.0 / LEVELS)

                def state(a):
                    word = fin[q, a * WORDS:(a + 1) * WORDS]
                    upper = lax.shift_right_arithmetic(word, jnp.int32(16))
                    lower = lax.bitwise_and(word, jnp.int32(65535)) - 32768
                    return jnp.concatenate([upper, lower], axis=0).astype(f32) * scales[a:a + 1]

                gradient = (gbuf[c, y, rows, cols] + grecv[c, 0, rows, cols]) + (
                    grecv[c, 1, rows, cols] + grecv[c, 2, rows, cols])
                old = state(0)
                first = beta_one * state(1) + (1.0 - beta_one) * gradient
                second = beta_two * state(2) + (1.0 - beta_two) * gradient * gradient
                update = first / (jnp.sqrt(second) + epsilon)
                gbuf[c, 0, rows, cols] = first
                gbuf[c, 1, rows, cols] = second
                gbuf[c, 2, rows, cols] = update
                gbuf[c, 3, rows, cols] = old
                norm[0:8] += jnp.sum((old * old).reshape(HIGH // 8, 8, LANES), axis=0)
                norm[8:16] += jnp.sum((update * update).reshape(HIGH // 8, 8, LANES), axis=0)

        put(new_1, c, 0).start()
        put(new_2, c, 1).start()

    def n_copy(o):
        return remote(norm, norm_in.at[o - 1], n_s.at[o], n_r.at[o], layer(o)[1])

    for o in range(1, NY):
        n_copy(o).start()
    for o in range(1, NY):
        n_copy(o).wait_recv()
    squares = (norm[...] + norm_in[0]) + (norm_in[1] + norm_in[2])
    weight_sq = jnp.sum(jnp.sum(squares[0:8], axis=0, keepdims=True), axis=1, keepdims=True)
    update_sq = jnp.sum(jnp.sum(squares[8:16], axis=0, keepdims=True), axis=1, keepdims=True)
    trust = jnp.sqrt(weight_sq) / (jnp.sqrt(update_sq) + epsilon)
    rate = learn_rate * trust
    for c in range(CHUNKS):
        gbuf[c, 3] = gbuf[c, 3] - rate * gbuf[c, 2]
        put(new_w, c, 3).start()

    for step in (1, 2, 3, 4):
        for d in (0, 1):
            if d in meta_steps(step):
                meta_copy(d, step).wait_send()
            tok_copy(d, step).wait_send()
            for c in range(CHUNKS):
                cot_copy(c, d, step).wait_send()
    all_pieces(upmid, 0).wait_send()
    all_pieces(upout, 2).wait_send()
    all_pieces(stg, 3).wait_send()
    for o in range(1, NY):
        up_copy(o).wait_send()
        n_copy(o).wait_send()
    for o in range(1, PLANE):
        for j in range(PAIRS):
            xt_copy(j, o).wait_send()
        for c in range(CHUNKS):
            xc_copy(c, o).wait_send()
    for c in range(CHUNKS):
        put(new_1, c, 0).wait()
        put(new_2, c, 1).wait()
        put(new_w, c, 3).wait()


def local(
    tokens, cotangent, expert_ids, gate_probs, up_weight, down_weight, moment1, moment2, pair_match
):
    rows, width = tokens.shape
    chunk = width // CHUNKS
    units = up_weight.shape[2]
    bf16, f32 = jnp.bfloat16, jnp.float32
    meta = jnp.concatenate([expert_ids.astype(f32).T, gate_probs.T], axis=0)
    up = up_weight[0].T
    pick = PLANE * 2 * CAP
    words = STATES * WORDS + 8
    dma = pltpu.SemaphoreType.DMA
    anywhere = pl.BlockSpec(memory_space=pl.ANY)
    outs = pl.pallas_call(
        step_kernel,
        out_shape=[jax.ShapeDtypeStruct((units, width), f32)] * 3,
        in_specs=[
            pl.BlockSpec(memory_space=pltpu.SMEM), pl.BlockSpec(memory_space=pltpu.VMEM),
        ] + [anywhere] * 6,
        out_specs=[anywhere] * 3,
        scratch_shapes=[
            pltpu.VMEM((NZ, rows, width), bf16),
            pltpu.VMEM((CHUNKS, NZ, rows, chunk), bf16),
            pltpu.VMEM((NZ,) + meta.shape, f32),
            pltpu.VMEM((PAIRS, pick, 2 * rows), bf16),
            pltpu.VMEM((PAIRS, pick, 1), f32),
            pltpu.VMEM((PAIRS, PLANE, 2 * CAP, width), bf16),
            pltpu.VMEM((CHUNKS, PLANE, PAIRS, 2 * CAP, chunk), bf16),
            pltpu.VMEM((PLANE, PAIRS, 2 * CAP, width), bf16),
            pltpu.VMEM((CHUNKS, PLANE, PAIRS, 2 * CAP, chunk), bf16),
            pltpu.VMEM((NY, units, width), bf16),
            pltpu.VMEM((NY * units, PAIRS * pick), bf16),
            pltpu.VMEM((CHUNKS, NY, units, chunk), f32),
            pltpu.VMEM((CHUNKS, NY - 1, units, chunk), f32),
            pltpu.VMEM((TOTAL, words, LANES), jnp.int32),
            pltpu.VMEM((TOTAL, words, LANES), jnp.int32),
            pltpu.VMEM((TOTAL, words, LANES), jnp.int32),
            pltpu.VMEM((TOTAL, HIGH, LANES), bf16),
            pltpu.VMEM((TOTAL, HIGH, LANES), bf16),
            pltpu.VMEM((16, LANES), f32),
            pltpu.VMEM((NY - 1, 16, LANES), f32),
            dma((2, 5)), dma((2, 5)),
            dma((2, 5)), dma((2, 5)),
            dma((CHUNKS, 2, 5)), dma((CHUNKS, 2, 5)),
            dma((NY,)), dma((NY,)),
            dma((PAIRS, PLANE)), dma((PAIRS, PLANE)),
            dma((CHUNKS, PLANE)), dma((CHUNKS, PLANE)),
            dma((CHUNKS, NY)), dma((CHUNKS, NY)),
            dma((NY,)), dma((NY,)),
            dma((4,)), dma((4,)),
            dma((2 + PAIRS + CHUNKS,)),
            dma((1 + CHUNKS + STATES * CHUNKS,)),
            dma((CHUNKS, 4)),
        ],
        compiler_params=pltpu.CompilerParams(
            collective_id=0, has_side_effects=True, vmem_limit_bytes=VMEM_BYTES
        ),
        cost_estimate=pl.CostEstimate(
            flops=4 * PAIRS * pick * width * units * NY,
            bytes_accessed=4 * rows * width + 26 * units * width,
            transcendentals=PAIRS * pick * units * NY,
        ),
    )(pair_match, meta, tokens, cotangent, up, down_weight[0], moment1[0], moment2[0])
    return tuple(out[None] for out in outs)


def solution(mesh):
    in_specs = (
        P(("dp", "expert"), None),
        P(("dp", "expert"), None),
        P(("dp", "expert"), None),
        P(("dp", "expert"), None),
        P("expert", None, "dp"),
        P("expert", "dp", None),
        P("expert", "dp", None),
        P("expert", "dp", None),
        P(),
    )
    out_specs = (P("expert", "dp", None), P("expert", "dp", None), P("expert", "dp", None))
    return jax.shard_map(local, mesh=mesh, in_specs=in_specs, out_specs=out_specs, check_vma=False)
```

```python
import jax
import jax.numpy as jnp
from jax import lax
from jax.experimental import pallas as pl
from jax.experimental.pallas import tpu as pltpu
from jax.sharding import PartitionSpec as P

beta_one = 0.9
beta_two = 0.999
epsilon = 1e-06
learn_rate = 0.05

NZ = 8
PLANE = 8
NY = 4
CAP = 24
TOK = 128
PAIRS = NZ // 2
CHUNKS = 4
SPREAD_AFTER = 3
GATHER_AFTER = 1
VMEM_BYTES = 62 * 2**20
TOTAL = NZ * PLANE
HIGH, LANES = 48, 128
ACROSS = 16
WORDS = HIGH // 2
STATES = 3
STEP = 0.6931471805599453 / 8.0
LEVELS = 32767.0
MESH = pl.DeviceIdType.MESH


def step_kernel(
    match, meta, tok, cot, up, weight, moment1, moment2, new_w, new_1, new_2,
    zt, zc, zm, sel, prob, sbt, sbs, rbt, rbs, upb, hid, gbuf, grecv,
    stg, mid, fin, upmid, upout, norm, norm_in,
    zt_s, zt_r, zm_s, zm_r, zc_s, zc_r, up_s, up_r, xt_s, xt_r, xc_s, xc_r, g_s, g_r, n_s, n_r,
    ex_s, ex_r, loc, load, store,
):
    f32, bf16, i32 = jnp.float32, jnp.bfloat16, jnp.int32
    width = tok.shape[1]
    chunk = width // CHUNKS
    per_chunk = chunk // LANES
    slice_rows = up.shape[0]
    groups = slice_rows // HIGH
    y = lax.axis_index("dp")
    e = lax.axis_index("expert")
    z = e // PLANE
    p = lax.rem(e, PLANE)
    right = (y, lax.rem(e + PLANE, TOTAL))
    left = (y, lax.rem(e + TOTAL - PLANE, TOTAL))

    def mate(o):
        q = lax.rem(p + o, PLANE)
        return q, (y, z * PLANE + q)

    def layer(o):
        k = lax.rem(y + o, NY)
        return k, (k, e)

    tok_load = pltpu.make_async_copy(tok, zt.at[0], load.at[0])
    tok_load.start()
    cot_loads = [
        pltpu.make_async_copy(cot.at[:, pl.ds(c * chunk, chunk)], zc.at[c, 0], load.at[1 + c])
        for c in range(CHUNKS)
    ]
    state_loads = [
        pltpu.make_async_copy(
            ref.at[:, pl.ds(c * chunk, chunk)], gbuf.at[a, c], load.at[1 + CHUNKS + a * CHUNKS + c])
        for a, ref in enumerate((weight, moment1, moment2)) for c in range(CHUNKS)
    ]
    for copy in state_loads + cot_loads:
        copy.start()
    zm[0] = meta[...]

    barrier = pltpu.get_barrier_semaphore()

    @pl.loop(1, TOTAL)
    def _(o):
        pl.semaphore_signal(
            barrier, inc=1, device_id=(y, lax.rem(e + o, TOTAL)), device_id_type=MESH)

    for o in range(1, NY):
        pl.semaphore_signal(barrier, inc=1, device_id=layer(o)[1], device_id_type=MESH)
    pl.semaphore_wait(barrier, TOTAL - 1 + NY - 1)

    def remote(src, dst, send, recv, device):
        return pltpu.make_async_remote_copy(
            src_ref=src, dst_ref=dst, send_sem=send, recv_sem=recv,
            device_id=device, device_id_type=MESH,
        )

    def held(direction, step):
        return 0 if step == 1 else 2 * (step - 1) + direction

    def landing(direction, step):
        return 1 if step == 4 else 2 * step + direction

    half = TOK // 2

    def z_copy(ring, send, recv, direction, step):
        src, dst = ring.at[held(direction, step)], ring.at[landing(direction, step)]
        if step == 4:
            rows = pl.ds(direction * half, half)
            src, dst = src.at[rows], dst.at[rows]
        return remote(src, dst, send.at[direction, step], recv.at[direction, step],
                      left if direction else right)

    def tok_copy(direction, step):
        return z_copy(zt, zt_s, zt_r, direction, step)

    def cot_copy(c, direction, step):
        return z_copy(zc.at[c], zc_s.at[c], zc_r.at[c], direction, step)

    def meta_copy(direction, step):
        return remote(zm.at[held(direction, step)], zm.at[landing(direction, step)],
                      zm_s.at[direction, step], zm_r.at[direction, step],
                      left if direction else right)

    def meta_steps(step):
        return (0,) if step == 4 else (0, 1)

    tok_load.wait()
    for d in (0, 1):
        meta_copy(d, 1).start()
        tok_copy(d, 1).start()

    def piece_of(q):
        rows = pl.ds(pl.multiple_of((q // ACROSS) * HIGH, HIGH), HIGH)
        cols = pl.ds(pl.multiple_of(lax.rem(q, ACROSS) * LANES, LANES), LANES)
        return rows, cols

    def all_pieces(buffer, index):
        span = pl.ds(0, TOTAL - 1)
        return remote(buffer.at[span], buffer.at[span], ex_s.at[index], ex_r.at[index], right)

    @pl.loop(1, TOTAL)
    def _(o):
        q = lax.rem(e + o, TOTAL)
        rows, cols = piece_of(q)
        remote(up.at[rows, cols], upmid.at[e], ex_s.at[0], ex_r.at[0], (y, q)).start()

    own_rows, own_cols = piece_of(e)
    own_up = pltpu.make_async_copy(up.at[own_rows, own_cols], upmid.at[e], loc.at[0])
    own_up.start()

    for c in range(CHUNKS):
        cot_loads[c].wait()
        for d in (0, 1):
            cot_copy(c, d, 1).start()

    scale_row = lax.broadcasted_iota(i32, (8, LANES), 0)
    for copy in state_loads:
        copy.wait()

    @pl.loop(0, CHUNKS)
    def _(c):
        for h in range(per_chunk):
            for g in range(groups):
                q = g * ACROSS + c * per_chunk + h
                powers = jnp.zeros((8, LANES), f32)
                for a in range(STATES):
                    x = gbuf[a, c, g * HIGH:(g + 1) * HIGH, h * LANES:(h + 1) * LANES]
                    most = jnp.maximum(jnp.max(jnp.abs(x), axis=0, keepdims=True), 1e-30)
                    power = jnp.ceil(jnp.log(most) * (1.0 / STEP))
                    inverse = 1.0 / (jnp.exp(power * STEP) * (1.0 / LEVELS))
                    code = jnp.clip(jnp.floor(x * inverse + 0.5), -LEVELS, LEVELS).astype(i32)
                    stg[q, a * WORDS:(a + 1) * WORDS] = code[:WORDS] * 65536 + (code[WORDS:] + 32768)
                    powers = jnp.where(scale_row == a, power, powers)
                stg[q, STATES * WORDS:] = powers.astype(i32)

    def up_copy(o):
        k, device = layer(o)
        return remote(upb.at[y], upb.at[y], up_s.at[o], up_r.at[o], device)

    row_of = lax.broadcasted_iota(i32, (TOK, TOK), 0)
    col_of = lax.broadcasted_iota(i32, (TOK, TOK), 1)
    before = (row_of < col_of).astype(f32).astype(bf16)
    place_of = lax.broadcasted_iota(i32, (PLANE, CAP, TOK), 1).astype(f32)
    which = lax.broadcasted_iota(i32, (PLANE, TOK), 0)
    expert_of = jnp.zeros((PLANE, TOK), i32)
    for k in range(PLANE):
        expert_of = jnp.where(which == k, match[z * PLANE + k], expert_of)
    expert_of = expert_of.astype(f32)

    def select_of(slot):
        mask = jnp.zeros((PLANE, TOK), f32)
        gates = jnp.zeros((PLANE, TOK), f32)
        top = meta.shape[0] // 2
        for k in range(top):
            hit = zm[slot, k:k + 1, :] == expert_of
            mask = jnp.where(hit, 1.0, mask)
            gates = jnp.where(hit, zm[slot, top + k:top + k + 1, :], gates)
        rank = jnp.dot(mask.astype(bf16), before, preferred_element_type=f32)
        rank = jnp.where(mask > 0.5, rank, -1.0)
        picked = jnp.where(rank[:, None, :] == place_of, 1.0, 0.0)
        gate = jnp.sum(picked * gates[:, None, :], axis=2, keepdims=True)
        return picked, gate

    def build(j):
        first_pick, first_gate = select_of(2 * j)
        second_pick, second_gate = select_of(2 * j + 1)
        blank = jnp.zeros((PLANE, CAP, TOK), f32)
        both = jnp.concatenate(
            [jnp.concatenate([first_pick, blank], axis=2),
             jnp.concatenate([blank, second_pick], axis=2)], axis=1)
        sel[j] = both.reshape(PLANE * 2 * CAP, 2 * TOK).astype(bf16)
        prob[j] = jnp.concatenate([first_gate, second_gate], axis=1).reshape(PLANE * 2 * CAP, 1)

    def xt_copy(j, o):
        q, device = mate(o)
        return remote(sbt.at[j, q], rbt.at[p, j], xt_s.at[j, o], xt_r.at[j, o], device)

    def xt_own(j):
        return pltpu.make_async_copy(sbt.at[j, p], rbt.at[p, j], loc.at[1 + j])

    def xc_copy(c, o):
        q, device = mate(o)
        return remote(sbs.at[c, q], rbs.at[c, p], xc_s.at[c, o], xc_r.at[c, o], device)

    def xc_own(c):
        return pltpu.make_async_copy(sbs.at[c, p], rbs.at[c, p], loc.at[1 + PAIRS + c])

    order = (4, 2, 6, 3, 5, 1, 7)

    def send_tokens(j):
        build(j)

        @pl.loop(0, CHUNKS)
        def _(c):
            cols = pl.ds(pl.multiple_of(c * chunk, chunk), chunk)
            pair = zt[2 * j:2 * j + 2, :, cols].reshape(2 * TOK, chunk)
            rows = jnp.dot(sel[j], pair, preferred_element_type=f32)
            sbt[j, :, :, cols] = rows.astype(bf16).reshape(PLANE, 2 * CAP, chunk)

        xt_own(j).start()
        for o in order:
            xt_copy(j, o).start()

    landed = upb.at[y, own_rows, own_cols]
    last_up = pltpu.make_async_copy(upout.at[e], landed, loc.at[1 + PAIRS + CHUNKS])

    for step in (1, 2, 3, 4):
        for d in (0, 1):
            if d in meta_steps(step):
                meta_copy(d, step).wait_recv()
                if step < 4 and d in meta_steps(step + 1):
                    meta_copy(d, step + 1).start()
            tok_copy(d, step).wait_recv()
            if step < 4:
                tok_copy(d, step + 1).start()
        send_tokens(0 if step == 4 else step)
        if step == 2:
            own_up.wait()
            all_pieces(upmid, 0).wait_recv()

            @pl.loop(0, TOTAL)
            def _(i):
                upout[i] = upmid[match[i]]

            @pl.loop(1, TOTAL)
            def _(o):
                q = lax.rem(e + o, TOTAL)
                remote(upout.at[q], landed, ex_s.at[2], ex_r.at[2], (y, q)).start()

            last_up.start()

    last_up.wait()
    all_pieces(upout, 2).wait_recv()
    for o in (2, 1, 3):
        up_copy(o).start()

    for step in (1, 2, 3, 4):
        for c in range(CHUNKS):
            for d in (0, 1):
                cot_copy(c, d, step).wait_recv()
                if step < 4:
                    cot_copy(c, d, step + 1).start()
            if step == 4:
                for j in range(PAIRS):
                    pair = zc[c, 2 * j:2 * j + 2].reshape(2 * TOK, chunk)
                    rows = jnp.dot(sel[j], pair, preferred_element_type=f32) * prob[j]
                    sbs[c, :, j] = rows.astype(bf16).reshape(PLANE, 2 * CAP, chunk)
                xc_own(c).start()
                for o in order:
                    xc_copy(c, o).start()
        if step == SPREAD_AFTER:
            @pl.loop(1, TOTAL)
            def _(o):
                q = lax.rem(e + o, TOTAL)
                remote(stg.at[q], mid.at[e], ex_s.at[1], ex_r.at[1], (y, q)).start()

            mid[e] = stg[e]

    for o in range(1, NY):
        up_copy(o).wait_recv()
    for j in range(PAIRS):
        xt_own(j).wait()
        for o in range(1, PLANE):
            xt_copy(j, o).wait_recv()
    span = 2 * PAIRS * 2 * CAP

    @pl.loop(0, PLANE // 2)
    def _(m):
        rows = rbt[pl.ds(2 * m, 2)].reshape(span, width)
        cols = pl.ds(pl.multiple_of(m * span, span), span)

        @pl.loop(0, NY)
        def _(k):
            v = lax.dot_general(upb[k], rows, (((1,), (1,)), ((), ())), preferred_element_type=f32)
            units = pl.ds(pl.multiple_of(k * slice_rows, slice_rows), slice_rows)
            hid[units, cols] = (v / (1.0 + jnp.exp(-v))).astype(bf16)

    def g_copy(c, o):
        k, device = layer(o)
        return remote(gbuf.at[c, k], grecv.at[c, o - 1], g_s.at[c, o], g_r.at[c, o], device)

    for c in range(CHUNKS):
        xc_own(c).wait()
        for o in range(1, PLANE):
            xc_copy(c, o).wait_recv()

        @pl.loop(0, NY)
        def _(k):
            units = pl.ds(pl.multiple_of(k * slice_rows, slice_rows), slice_rows)
            rows = rbs[c].reshape(PLANE * PAIRS * 2 * CAP, chunk)
            gbuf[c, k] = jnp.dot(hid[units, :], rows, preferred_element_type=f32)

        for o in (2, 1, 3):
            g_copy(c, o).start()
        if c == GATHER_AFTER:
            all_pieces(stg, 1).wait_send()
            all_pieces(mid, 1).wait_recv()

            @pl.loop(0, TOTAL)
            def _(i):
                stg[i] = mid[match[i]]

            @pl.loop(1, TOTAL)
            def _(o):
                q = lax.rem(e + o, TOTAL)
                remote(stg.at[q], fin.at[e], ex_s.at[3], ex_r.at[3], (y, q)).start()

            fin[e] = stg[e]

    all_pieces(fin, 3).wait_recv()
    norm[...] = jnp.zeros_like(norm)

    def put(ref, c, slot):
        return pltpu.make_async_copy(
            gbuf.at[c, slot], ref.at[:, pl.ds(c * chunk, chunk)], store.at[c, slot])

    for c in range(CHUNKS):
        for o in range(1, NY):
            g_copy(c, o).wait()

        @pl.loop(0, groups)
        def _(g):
            rows = pl.ds(pl.multiple_of(g * HIGH, HIGH), HIGH)
            for h in range(per_chunk):
                q = g * ACROSS + c * per_chunk + h
                cols = slice(h * LANES, (h + 1) * LANES)
                powers = fin[q, STATES * WORDS:].astype(f32)
                scales = jnp.exp(powers * STEP) * (1.0 / LEVELS)

                def state(a):
                    word = fin[q, a * WORDS:(a + 1) * WORDS]
                    upper = lax.shift_right_arithmetic(word, jnp.int32(16))
                    lower = lax.bitwise_and(word, jnp.int32(65535)) - 32768
                    return jnp.concatenate([upper, lower], axis=0).astype(f32) * scales[a:a + 1]

                gradient = (gbuf[c, y, rows, cols] + grecv[c, 0, rows, cols]) + (
                    grecv[c, 1, rows, cols] + grecv[c, 2, rows, cols])
                old = state(0)
                first = beta_one * state(1) + (1.0 - beta_one) * gradient
                second = beta_two * state(2) + (1.0 - beta_two) * gradient * gradient
                update = first / (jnp.sqrt(second) + epsilon)
                gbuf[c, 0, rows, cols] = first
                gbuf[c, 1, rows, cols] = second
                gbuf[c, 2, rows, cols] = update
                gbuf[c, 3, rows, cols] = old
                norm[0:8] += jnp.sum((old * old).reshape(HIGH // 8, 8, LANES), axis=0)
                norm[8:16] += jnp.sum((update * update).reshape(HIGH // 8, 8, LANES), axis=0)

        put(new_1, c, 0).start()
        put(new_2, c, 1).start()

    def n_copy(o):
        return remote(norm, norm_in.at[o - 1], n_s.at[o], n_r.at[o], layer(o)[1])

    for o in range(1, NY):
        n_copy(o).start()
    for o in range(1, NY):
        n_copy(o).wait_recv()
    squares = (norm[...] + norm_in[0]) + (norm_in[1] + norm_in[2])
    weight_sq = jnp.sum(jnp.sum(squares[0:8], axis=0, keepdims=True), axis=1, keepdims=True)
    update_sq = jnp.sum(jnp.sum(squares[8:16], axis=0, keepdims=True), axis=1, keepdims=True)
    trust = jnp.sqrt(weight_sq) / (jnp.sqrt(update_sq) + epsilon)
    rate = learn_rate * trust
    for c in range(CHUNKS):
        gbuf[c, 3] = gbuf[c, 3] - rate * gbuf[c, 2]
        put(new_w, c, 3).start()

    for step in (1, 2, 3, 4):
        for d in (0, 1):
            if d in meta_steps(step):
                meta_copy(d, step).wait_send()
            tok_copy(d, step).wait_send()
            for c in range(CHUNKS):
                cot_copy(c, d, step).wait_send()
    all_pieces(upmid, 0).wait_send()
    all_pieces(upout, 2).wait_send()
    all_pieces(stg, 3).wait_send()
    for o in range(1, NY):
        up_copy(o).wait_send()
        n_copy(o).wait_send()
    for o in range(1, PLANE):
        for j in range(PAIRS):
            xt_copy(j, o).wait_send()
        for c in range(CHUNKS):
            xc_copy(c, o).wait_send()
    for c in range(CHUNKS):
        put(new_1, c, 0).wait()
        put(new_2, c, 1).wait()
        put(new_w, c, 3).wait()


def local(
    tokens, cotangent, expert_ids, gate_probs, up_weight, down_weight, moment1, moment2, pair_match
):
    rows, width = tokens.shape
    chunk = width // CHUNKS
    units = up_weight.shape[2]
    bf16, f32 = jnp.bfloat16, jnp.float32
    meta = jnp.concatenate([expert_ids.astype(f32).T, gate_probs.T], axis=0)
    up = up_weight[0].T
    pick = PLANE * 2 * CAP
    words = STATES * WORDS + 8
    dma = pltpu.SemaphoreType.DMA
    anywhere = pl.BlockSpec(memory_space=pl.ANY)
    outs = pl.pallas_call(
        step_kernel,
        out_shape=[jax.ShapeDtypeStruct((units, width), f32)] * 3,
        in_specs=[
            pl.BlockSpec(memory_space=pltpu.SMEM), pl.BlockSpec(memory_space=pltpu.VMEM),
        ] + [anywhere] * 6,
        out_specs=[anywhere] * 3,
        scratch_shapes=[
            pltpu.VMEM((NZ, rows, width), bf16),
            pltpu.VMEM((CHUNKS, NZ, rows, chunk), bf16),
            pltpu.VMEM((NZ,) + meta.shape, f32),
            pltpu.VMEM((PAIRS, pick, 2 * rows), bf16),
            pltpu.VMEM((PAIRS, pick, 1), f32),
            pltpu.VMEM((PAIRS, PLANE, 2 * CAP, width), bf16),
            pltpu.VMEM((CHUNKS, PLANE, PAIRS, 2 * CAP, chunk), bf16),
            pltpu.VMEM((PLANE, PAIRS, 2 * CAP, width), bf16),
            pltpu.VMEM((CHUNKS, PLANE, PAIRS, 2 * CAP, chunk), bf16),
            pltpu.VMEM((NY, units, width), bf16),
            pltpu.VMEM((NY * units, PAIRS * pick), bf16),
            pltpu.VMEM((CHUNKS, NY, units, chunk), f32),
            pltpu.VMEM((CHUNKS, NY - 1, units, chunk), f32),
            pltpu.VMEM((TOTAL, words, LANES), jnp.int32),
            pltpu.VMEM((TOTAL, words, LANES), jnp.int32),
            pltpu.VMEM((TOTAL, words, LANES), jnp.int32),
            pltpu.VMEM((TOTAL, HIGH, LANES), bf16),
            pltpu.VMEM((TOTAL, HIGH, LANES), bf16),
            pltpu.VMEM((16, LANES), f32),
            pltpu.VMEM((NY - 1, 16, LANES), f32),
            dma((2, 5)), dma((2, 5)),
            dma((2, 5)), dma((2, 5)),
            dma((CHUNKS, 2, 5)), dma((CHUNKS, 2, 5)),
            dma((NY,)), dma((NY,)),
            dma((PAIRS, PLANE)), dma((PAIRS, PLANE)),
            dma((CHUNKS, PLANE)), dma((CHUNKS, PLANE)),
            dma((CHUNKS, NY)), dma((CHUNKS, NY)),
            dma((NY,)), dma((NY,)),
            dma((4,)), dma((4,)),
            dma((2 + PAIRS + CHUNKS,)),
            dma((1 + CHUNKS + STATES * CHUNKS,)),
            dma((CHUNKS, 4)),
        ],
        compiler_params=pltpu.CompilerParams(
            collective_id=0, has_side_effects=True, vmem_limit_bytes=VMEM_BYTES
        ),
        cost_estimate=pl.CostEstimate(
            flops=4 * PAIRS * pick * width * units * NY,
            bytes_accessed=4 * rows * width + 26 * units * width,
            transcendentals=PAIRS * pick * units * NY,
        ),
    )(pair_match, meta, tokens, cotangent, up, down_weight[0], moment1[0], moment2[0])
    return tuple(out[None] for out in outs)


def solution(mesh):
    in_specs = (
        P(("dp", "expert"), None),
        P(("dp", "expert"), None),
        P(("dp", "expert"), None),
        P(("dp", "expert"), None),
        P("expert", None, "dp"),
        P("expert", "dp", None),
        P("expert", "dp", None),
        P("expert", "dp", None),
        P(),
    )
    out_specs = (P("expert", "dp", None), P("expert", "dp", None), P("expert", "dp", None))
    return jax.shard_map(local, mesh=mesh, in_specs=in_specs, out_specs=out_specs, check_vma=False)
```

```python
import jax
import jax.numpy as jnp
from jax import lax
from jax.experimental import pallas as pl
from jax.experimental.pallas import tpu as pltpu
from jax.sharding import PartitionSpec as P

beta_one = 0.9
beta_two = 0.999
epsilon = 1e-06
learn_rate = 0.05

NZ = 8
PLANE = 8
NY = 4
CAP = 24
TOK = 128
PAIRS = NZ // 2
CHUNKS = 8
RING = 4
PARTS = 2
SPREAD_AFTER = 3
GATHER_AFTER = 3
VMEM_BYTES = 62 * 2**20
TOTAL = NZ * PLANE
HIGH, LANES = 48, 128
ACROSS = 16
WORDS = HIGH // 2
STATES = 3
STEP = 0.6931471805599453 / 8.0
LEVELS = 32767.0
MESH = pl.DeviceIdType.MESH


def step_kernel(
    match, meta, tok, cot, up, weight, moment1, moment2, new_w, new_1, new_2,
    zt, zc, zm, sel, prob, sbt, sbs, rbt, rbs, upb, hid, gbuf, grecv,
    stg, mid, fin, upmid, upout, norm, norm_in,
    zt_s, zt_r, zm_s, zm_r, zc_s, zc_r, up_s, up_r, xt_s, xt_r, xc_s, xc_r, g_s, g_r, n_s, n_r,
    ex_s, ex_r, loc, load, store,
):
    f32, bf16, i32 = jnp.float32, jnp.bfloat16, jnp.int32
    width = tok.shape[1]
    chunk = width // CHUNKS
    per_chunk = chunk // LANES
    ring_cols = width // RING
    part = width // PARTS
    slice_rows = up.shape[0]
    groups = slice_rows // HIGH
    y = lax.axis_index("dp")
    e = lax.axis_index("expert")
    z = e // PLANE
    p = lax.rem(e, PLANE)
    right = (y, lax.rem(e + PLANE, TOTAL))
    left = (y, lax.rem(e + TOTAL - PLANE, TOTAL))

    def mate(o):
        q = lax.rem(p + o, PLANE)
        return q, (y, z * PLANE + q)

    def layer(o):
        k = lax.rem(y + o, NY)
        return k, (k, e)

    tok_loads = [
        pltpu.make_async_copy(tok.at[:, pl.ds(t * part, part)], zt.at[t, 0], load.at[t])
        for t in range(PARTS)
    ]
    for copy in tok_loads:
        copy.start()
    cot_loads = [
        pltpu.make_async_copy(
            cot.at[:, pl.ds(c * ring_cols, ring_cols)], zc.at[c, 0], load.at[PARTS + c])
        for c in range(RING)
    ]
    state_loads = [
        pltpu.make_async_copy(
            ref.at[:, pl.ds(c * chunk, chunk)],
            gbuf.at[(a * CHUNKS + c) // NY, (a * CHUNKS + c) % NY],
            load.at[PARTS + RING + a * CHUNKS + c])
        for a, ref in enumerate((weight, moment1, moment2)) for c in range(CHUNKS)
    ]
    for copy in state_loads + cot_loads:
        copy.start()
    zm[0] = meta[...]

    barrier = pltpu.get_barrier_semaphore()

    @pl.loop(1, TOTAL)
    def _(o):
        pl.semaphore_signal(
            barrier, inc=1, device_id=(y, lax.rem(e + o, TOTAL)), device_id_type=MESH)

    for o in range(1, NY):
        pl.semaphore_signal(barrier, inc=1, device_id=layer(o)[1], device_id_type=MESH)
    pl.semaphore_wait(barrier, TOTAL - 1 + NY - 1)

    def remote(src, dst, send, recv, device):
        return pltpu.make_async_remote_copy(
            src_ref=src, dst_ref=dst, send_sem=send, recv_sem=recv,
            device_id=device, device_id_type=MESH,
        )

    def held(direction, step):
        return 0 if step == 1 else 2 * (step - 1) + direction

    def landing(direction, step):
        return 1 if step == 4 else 2 * step + direction

    half = TOK // 2

    def z_copy(ring, send, recv, direction, step):
        src, dst = ring.at[held(direction, step)], ring.at[landing(direction, step)]
        if step == 4:
            rows = pl.ds(direction * half, half)
            src, dst = src.at[rows], dst.at[rows]
        return remote(src, dst, send.at[direction, step], recv.at[direction, step],
                      left if direction else right)

    def tok_copy(t, direction, step):
        return z_copy(zt.at[t], zt_s.at[t], zt_r.at[t], direction, step)

    def cot_copy(c, direction, step):
        return z_copy(zc.at[c], zc_s.at[c], zc_r.at[c], direction, step)

    def meta_copy(direction, step):
        return remote(zm.at[held(direction, step)], zm.at[landing(direction, step)],
                      zm_s.at[direction, step], zm_r.at[direction, step],
                      left if direction else right)

    def meta_steps(step):
        return (0,) if step == 4 else (0, 1)

    for d in (0, 1):
        meta_copy(d, 1).start()
    for t in range(PARTS):
        tok_loads[t].wait()
        for d in (0, 1):
            tok_copy(t, d, 1).start()

    def piece_of(q):
        rows = pl.ds(pl.multiple_of((q // ACROSS) * HIGH, HIGH), HIGH)
        cols = pl.ds(pl.multiple_of(lax.rem(q, ACROSS) * LANES, LANES), LANES)
        return rows, cols

    def all_pieces(buffer, index):
        span = pl.ds(0, TOTAL - 1)
        return remote(buffer.at[span], buffer.at[span], ex_s.at[index], ex_r.at[index], right)

    @pl.loop(1, TOTAL)
    def _(o):
        q = lax.rem(e + o, TOTAL)
        rows, cols = piece_of(q)
        remote(up.at[rows, cols], upmid.at[e], ex_s.at[0], ex_r.at[0], (y, q)).start()

    own_rows, own_cols = piece_of(e)
    own_up = pltpu.make_async_copy(up.at[own_rows, own_cols], upmid.at[e], loc.at[0])
    own_up.start()

    for c in range(RING):
        cot_loads[c].wait()
        for d in (0, 1):
            cot_copy(c, d, 1).start()

    scale_row = lax.broadcasted_iota(i32, (8, LANES), 0)
    for copy in state_loads:
        copy.wait()

    @pl.loop(0, CHUNKS)
    def _(c):
        for h in range(per_chunk):
            for g in range(groups):
                q = g * ACROSS + c * per_chunk + h
                powers = jnp.zeros((8, LANES), f32)
                for a in range(STATES):
                    x = gbuf[(a * CHUNKS + c) // NY, lax.rem(a * CHUNKS + c, NY), g * HIGH:(g + 1) * HIGH, h * LANES:(h + 1) * LANES]
                    most = jnp.maximum(jnp.max(jnp.abs(x), axis=0, keepdims=True), 1e-30)
                    power = jnp.ceil(jnp.log(most) * (1.0 / STEP))
                    inverse = 1.0 / (jnp.exp(power * STEP) * (1.0 / LEVELS))
                    code = jnp.clip(jnp.floor(x * inverse + 0.5), -LEVELS, LEVELS).astype(i32)
                    stg[q, a * WORDS:(a + 1) * WORDS] = code[:WORDS] * 65536 + (code[WORDS:] + 32768)
                    powers = jnp.where(scale_row == a, power, powers)
                stg[q, STATES * WORDS:] = powers.astype(i32)

    def up_copy(o):
        k, device = layer(o)
        return remote(upb.at[y], upb.at[y], up_s.at[o], up_r.at[o], device)

    row_of = lax.broadcasted_iota(i32, (TOK, TOK), 0)
    col_of = lax.broadcasted_iota(i32, (TOK, TOK), 1)
    before = (row_of < col_of).astype(f32).astype(bf16)
    place_of = lax.broadcasted_iota(i32, (PLANE, CAP, TOK), 1).astype(f32)
    which = lax.broadcasted_iota(i32, (PLANE, TOK), 0)
    expert_of = jnp.zeros((PLANE, TOK), i32)
    for k in range(PLANE):
        expert_of = jnp.where(which == k, match[z * PLANE + k], expert_of)
    expert_of = expert_of.astype(f32)

    def select_of(slot):
        mask = jnp.zeros((PLANE, TOK), f32)
        gates = jnp.zeros((PLANE, TOK), f32)
        top = meta.shape[0] // 2
        for k in range(top):
            hit = zm[slot, k:k + 1, :] == expert_of
            mask = jnp.where(hit, 1.0, mask)
            gates = jnp.where(hit, zm[slot, top + k:top + k + 1, :], gates)
        rank = jnp.dot(mask.astype(bf16), before, preferred_element_type=f32)
        rank = jnp.where(mask > 0.5, rank, -1.0)
        picked = jnp.where(rank[:, None, :] == place_of, 1.0, 0.0)
        gate = jnp.sum(picked * gates[:, None, :], axis=2, keepdims=True)
        return picked, gate

    def build(j):
        first_pick, first_gate = select_of(2 * j)
        second_pick, second_gate = select_of(2 * j + 1)
        blank = jnp.zeros((PLANE, CAP, TOK), f32)
        both = jnp.concatenate(
            [jnp.concatenate([first_pick, blank], axis=2),
             jnp.concatenate([blank, second_pick], axis=2)], axis=1)
        sel[j] = both.reshape(PLANE * 2 * CAP, 2 * TOK).astype(bf16)
        prob[j] = jnp.concatenate([first_gate, second_gate], axis=1).reshape(PLANE * 2 * CAP, 1)

    def xt_copy(j, t, o):
        q, device = mate(o)
        cols = pl.ds(t * part, part)
        return remote(sbt.at[j, q, :, cols], rbt.at[p, j, :, cols],
                      xt_s.at[j, t, o], xt_r.at[j, t, o], device)

    def xt_own(j):
        return pltpu.make_async_copy(sbt.at[j, p], rbt.at[p, j], loc.at[1 + j])

    def xc_copy(c, o):
        q, device = mate(o)
        return remote(sbs.at[c, q], rbs.at[c, p], xc_s.at[c, o], xc_r.at[c, o], device)

    def xc_own(c):
        return pltpu.make_async_copy(sbs.at[c, p], rbs.at[c, p], loc.at[1 + PAIRS + c])

    order = (4, 2, 6, 3, 5, 1, 7)

    def send_tokens(j, t):
        @pl.loop(0, part // 512)
        def _(c):
            cols = pl.ds(pl.multiple_of(c * 512, 512), 512)
            pair = zt[t, 2 * j:2 * j + 2, :, cols].reshape(2 * TOK, 512)
            rows = jnp.dot(sel[j], pair, preferred_element_type=f32)
            there = pl.ds(pl.multiple_of(t * part + c * 512, 512), 512)
            sbt[j, :, :, there] = rows.astype(bf16).reshape(PLANE, 2 * CAP, 512)

        for o in order:
            xt_copy(j, t, o).start()

    landed = upb.at[y, own_rows, own_cols]
    last_up = pltpu.make_async_copy(upout.at[e], landed, loc.at[1 + PAIRS + CHUNKS])

    for step in (1, 2, 3, 4):
        for d in (0, 1):
            if d in meta_steps(step):
                meta_copy(d, step).wait_recv()
                if step < 4 and d in meta_steps(step + 1):
                    meta_copy(d, step + 1).start()
        j = 0 if step == 4 else step
        for t in range(PARTS):
            for d in (0, 1):
                tok_copy(t, d, step).wait_recv()
                if step < 4:
                    tok_copy(t, d, step + 1).start()
            if t == 0:
                build(j)
            send_tokens(j, t)
        xt_own(j).start()
        if step == 2:
            own_up.wait()
            all_pieces(upmid, 0).wait_recv()

            @pl.loop(0, TOTAL)
            def _(i):
                upout[i] = upmid[match[i]]

            @pl.loop(1, TOTAL)
            def _(o):
                q = lax.rem(e + o, TOTAL)
                remote(upout.at[q], landed, ex_s.at[2], ex_r.at[2], (y, q)).start()

            last_up.start()

    last_up.wait()
    all_pieces(upout, 2).wait_recv()
    for o in (2, 1, 3):
        up_copy(o).start()

    for step in (1, 2, 3, 4):
        for r in range(RING):
            for d in (0, 1):
                cot_copy(r, d, step).wait_recv()
                if step < 4:
                    cot_copy(r, d, step + 1).start()
            ratio = CHUNKS // RING
            for c in range(r * ratio, (r + 1) * ratio) if step == 4 else ():
                across = slice((c % ratio) * chunk, (c % ratio + 1) * chunk)
                for j in range(PAIRS):
                    pair = zc[r, 2 * j:2 * j + 2, :, across].reshape(2 * TOK, chunk)
                    rows = jnp.dot(sel[j], pair, preferred_element_type=f32) * prob[j]
                    sbs[c, :, j] = rows.astype(bf16).reshape(PLANE, 2 * CAP, chunk)
                xc_own(c).start()
                for o in order:
                    xc_copy(c, o).start()
        if step == SPREAD_AFTER:
            @pl.loop(1, TOTAL)
            def _(o):
                q = lax.rem(e + o, TOTAL)
                remote(stg.at[q], mid.at[e], ex_s.at[1], ex_r.at[1], (y, q)).start()

            mid[e] = stg[e]

    for o in range(1, NY):
        up_copy(o).wait_recv()
    for j in range(PAIRS):
        xt_own(j).wait()
        for o in range(1, PLANE):
            for t in range(PARTS):
                xt_copy(j, t, o).wait_recv()
    span = 2 * PAIRS * 2 * CAP

    @pl.loop(0, PLANE // 2)
    def _(m):
        rows = rbt[pl.ds(2 * m, 2)].reshape(span, width)
        cols = pl.ds(pl.multiple_of(m * span, span), span)

        @pl.loop(0, NY)
        def _(k):
            v = lax.dot_general(upb[k], rows, (((1,), (1,)), ((), ())), preferred_element_type=f32)
            units = pl.ds(pl.multiple_of(k * slice_rows, slice_rows), slice_rows)
            hid[units, cols] = (v / (1.0 + jnp.exp(-v))).astype(bf16)

    def g_copy(c, o):
        k, device = layer(o)
        return remote(gbuf.at[c, k], grecv.at[c, o - 1], g_s.at[c, o], g_r.at[c, o], device)

    for c in range(CHUNKS):
        xc_own(c).wait()
        for o in range(1, PLANE):
            xc_copy(c, o).wait_recv()

        @pl.loop(0, NY)
        def _(k):
            units = pl.ds(pl.multiple_of(k * slice_rows, slice_rows), slice_rows)
            rows = rbs[c].reshape(PLANE * PAIRS * 2 * CAP, chunk)
            gbuf[c, k] = jnp.dot(hid[units, :], rows, preferred_element_type=f32)

        for o in (2, 1, 3):
            g_copy(c, o).start()
        if c == GATHER_AFTER:
            all_pieces(stg, 1).wait_send()
            all_pieces(mid, 1).wait_recv()

            @pl.loop(0, TOTAL)
            def _(i):
                stg[i] = mid[match[i]]

            @pl.loop(1, TOTAL)
            def _(o):
                q = lax.rem(e + o, TOTAL)
                remote(stg.at[q], fin.at[e], ex_s.at[3], ex_r.at[3], (y, q)).start()

            fin[e] = stg[e]

    all_pieces(fin, 3).wait_recv()
    norm[...] = jnp.zeros_like(norm)

    def put(ref, c, slot):
        return pltpu.make_async_copy(
            gbuf.at[c, slot], ref.at[:, pl.ds(c * chunk, chunk)], store.at[c, slot])

    for c in range(CHUNKS):
        for o in range(1, NY):
            g_copy(c, o).wait()

        @pl.loop(0, groups)
        def _(g):
            rows = pl.ds(pl.multiple_of(g * HIGH, HIGH), HIGH)
            for h in range(per_chunk):
                q = g * ACROSS + c * per_chunk + h
                cols = slice(h * LANES, (h + 1) * LANES)
                powers = fin[q, STATES * WORDS:].astype(f32)
                scales = jnp.exp(powers * STEP) * (1.0 / LEVELS)

                def state(a):
                    word = fin[q, a * WORDS:(a + 1) * WORDS]
                    upper = lax.shift_right_arithmetic(word, jnp.int32(16))
                    lower = lax.bitwise_and(word, jnp.int32(65535)) - 32768
                    return jnp.concatenate([upper, lower], axis=0).astype(f32) * scales[a:a + 1]

                gradient = (gbuf[c, y, rows, cols] + grecv[c, 0, rows, cols]) + (
                    grecv[c, 1, rows, cols] + grecv[c, 2, rows, cols])
                old = state(0)
                first = beta_one * state(1) + (1.0 - beta_one) * gradient
                second = beta_two * state(2) + (1.0 - beta_two) * gradient * gradient
                update = first / (jnp.sqrt(second) + epsilon)
                gbuf[c, 0, rows, cols] = first
                gbuf[c, 1, rows, cols] = second
                gbuf[c, 2, rows, cols] = update
                gbuf[c, 3, rows, cols] = old
                norm[0:8] += jnp.sum((old * old).reshape(HIGH // 8, 8, LANES), axis=0)
                norm[8:16] += jnp.sum((update * update).reshape(HIGH // 8, 8, LANES), axis=0)

        put(new_1, c, 0).start()
        put(new_2, c, 1).start()

    def n_copy(o):
        return remote(norm, norm_in.at[o - 1], n_s.at[o], n_r.at[o], layer(o)[1])

    for o in range(1, NY):
        n_copy(o).start()
    for o in range(1, NY):
        n_copy(o).wait_recv()
    squares = (norm[...] + norm_in[0]) + (norm_in[1] + norm_in[2])
    weight_sq = jnp.sum(jnp.sum(squares[0:8], axis=0, keepdims=True), axis=1, keepdims=True)
    update_sq = jnp.sum(jnp.sum(squares[8:16], axis=0, keepdims=True), axis=1, keepdims=True)
    trust = jnp.sqrt(weight_sq) / (jnp.sqrt(update_sq) + epsilon)
    rate = learn_rate * trust
    for c in range(CHUNKS):
        gbuf[c, 3] = gbuf[c, 3] - rate * gbuf[c, 2]
        put(new_w, c, 3).start()

    for step in (1, 2, 3, 4):
        for d in (0, 1):
            if d in meta_steps(step):
                meta_copy(d, step).wait_send()
            for t in range(PARTS):
                tok_copy(t, d, step).wait_send()
            for c in range(RING):
                cot_copy(c, d, step).wait_send()
    all_pieces(upmid, 0).wait_send()
    all_pieces(upout, 2).wait_send()
    all_pieces(stg, 3).wait_send()
    for o in range(1, NY):
        up_copy(o).wait_send()
        n_copy(o).wait_send()
    for o in range(1, PLANE):
        for j in range(PAIRS):
            for t in range(PARTS):
                xt_copy(j, t, o).wait_send()
        for c in range(CHUNKS):
            xc_copy(c, o).wait_send()
    for c in range(CHUNKS):
        put(new_1, c, 0).wait()
        put(new_2, c, 1).wait()
        put(new_w, c, 3).wait()


def local(
    tokens, cotangent, expert_ids, gate_probs, up_weight, down_weight, moment1, moment2, pair_match
):
    rows, width = tokens.shape
    chunk = width // CHUNKS
    units = up_weight.shape[2]
    bf16, f32 = jnp.bfloat16, jnp.float32
    meta = jnp.concatenate([expert_ids.astype(f32).T, gate_probs.T], axis=0)
    up = up_weight[0].T
    pick = PLANE * 2 * CAP
    words = STATES * WORDS + 8
    dma = pltpu.SemaphoreType.DMA
    anywhere = pl.BlockSpec(memory_space=pl.ANY)
    outs = pl.pallas_call(
        step_kernel,
        out_shape=[jax.ShapeDtypeStruct((units, width), f32)] * 3,
        in_specs=[
            pl.BlockSpec(memory_space=pltpu.SMEM), pl.BlockSpec(memory_space=pltpu.VMEM),
        ] + [anywhere] * 6,
        out_specs=[anywhere] * 3,
        scratch_shapes=[
            pltpu.VMEM((PARTS, NZ, rows, width // PARTS), bf16),
            pltpu.VMEM((RING, NZ, rows, width // RING), bf16),
            pltpu.VMEM((NZ,) + meta.shape, f32),
            pltpu.VMEM((PAIRS, pick, 2 * rows), bf16),
            pltpu.VMEM((PAIRS, pick, 1), f32),
            pltpu.VMEM((PAIRS, PLANE, 2 * CAP, width), bf16),
            pltpu.VMEM((CHUNKS, PLANE, PAIRS, 2 * CAP, chunk), bf16),
            pltpu.VMEM((PLANE, PAIRS, 2 * CAP, width), bf16),
            pltpu.VMEM((CHUNKS, PLANE, PAIRS, 2 * CAP, chunk), bf16),
            pltpu.VMEM((NY, units, width), bf16),
            pltpu.VMEM((NY * units, PAIRS * pick), bf16),
            pltpu.VMEM((CHUNKS, NY, units, chunk), f32),
            pltpu.VMEM((CHUNKS, NY - 1, units, chunk), f32),
            pltpu.VMEM((TOTAL, words, LANES), jnp.int32),
            pltpu.VMEM((TOTAL, words, LANES), jnp.int32),
            pltpu.VMEM((TOTAL, words, LANES), jnp.int32),
            pltpu.VMEM((TOTAL, HIGH, LANES), bf16),
            pltpu.VMEM((TOTAL, HIGH, LANES), bf16),
            pltpu.VMEM((16, LANES), f32),
            pltpu.VMEM((NY - 1, 16, LANES), f32),
            dma((PARTS, 2, 5)), dma((PARTS, 2, 5)),
            dma((2, 5)), dma((2, 5)),
            dma((RING, 2, 5)), dma((RING, 2, 5)),
            dma((NY,)), dma((NY,)),
            dma((PAIRS, PARTS, PLANE)), dma((PAIRS, PARTS, PLANE)),
            dma((CHUNKS, PLANE)), dma((CHUNKS, PLANE)),
            dma((CHUNKS, NY)), dma((CHUNKS, NY)),
            dma((NY,)), dma((NY,)),
            dma((4,)), dma((4,)),
            dma((2 + PAIRS + CHUNKS,)),
            dma((PARTS + RING + STATES * CHUNKS,)),
            dma((CHUNKS, 4)),
        ],
        compiler_params=pltpu.CompilerParams(
            collective_id=0, has_side_effects=True, vmem_limit_bytes=VMEM_BYTES
        ),
        cost_estimate=pl.CostEstimate(
            flops=4 * PAIRS * pick * width * units * NY,
            bytes_accessed=4 * rows * width + 26 * units * width,
            transcendentals=PAIRS * pick * units * NY,
        ),
    )(pair_match, meta, tokens, cotangent, up, down_weight[0], moment1[0], moment2[0])
    return tuple(out[None] for out in outs)


def solution(mesh):
    in_specs = (
        P(("dp", "expert"), None),
        P(("dp", "expert"), None),
        P(("dp", "expert"), None),
        P(("dp", "expert"), None),
        P("expert", None, "dp"),
        P("expert", "dp", None),
        P("expert", "dp", None),
        P("expert", "dp", None),
        P(),
    )
    out_specs = (P("expert", "dp", None), P("expert", "dp", None), P("expert", "dp", None))
    return jax.shard_map(local, mesh=mesh, in_specs=in_specs, out_specs=out_specs, check_vma=False)
```

```python
import jax
import jax.numpy as jnp
from jax import lax
from jax.experimental import pallas as pl
from jax.experimental.pallas import tpu as pltpu
from jax.sharding import PartitionSpec as P

beta_one = 0.9
beta_two = 0.999
epsilon = 1e-06
learn_rate = 0.05

NZ = 8
PLANE = 8
NY = 4
CAP = 24
TOK = 128
PAIRS = NZ // 2
CHUNKS = 8
RING = 4
PARTS = 2
SPREAD_AFTER = 3
GATHER_AFTER = 3
VMEM_BYTES = 62 * 2**20
TOTAL = NZ * PLANE
HIGH, LANES = 48, 128
ACROSS = 16
WORDS = HIGH // 2
STATES = 3
STEP = 0.6931471805599453 / 8.0
LEVELS = 32767.0
SMALLEST = 2.0**-63
MESH = pl.DeviceIdType.MESH


def step_kernel(
    match, ids, gates, tok, cot, up, weight, moment1, moment2, new_w, new_1, new_2,
    zt, zc, zm, sel, prob, sbt, sbs, rbt, rbs, upb, hid, gbuf, grecv,
    stg, mid, fin, upmid, upout, norm, norm_in,
    zt_s, zt_r, zm_s, zm_r, zc_s, zc_r, up_s, up_r, xt_s, xt_r, xc_s, xc_r, g_s, g_r, n_s, n_r,
    ex_s, ex_r, loc, load, store,
):
    f32, bf16, i32 = jnp.float32, jnp.bfloat16, jnp.int32
    width = tok.shape[1]
    chunk = width // CHUNKS
    per_chunk = chunk // LANES
    ring_cols = width // RING
    part = width // PARTS
    slice_rows = up.shape[0]
    groups = slice_rows // HIGH
    y = lax.axis_index("dp")
    e = lax.axis_index("expert")
    z = e // PLANE
    p = lax.rem(e, PLANE)
    right = (y, lax.rem(e + PLANE, TOTAL))
    left = (y, lax.rem(e + TOTAL - PLANE, TOTAL))

    def mate(o):
        q = lax.rem(p + o, PLANE)
        return q, (y, z * PLANE + q)

    def layer(o):
        k = lax.rem(y + o, NY)
        return k, (k, e)

    tok_loads = [
        pltpu.make_async_copy(tok.at[:, pl.ds(t * part, part)], zt.at[t, 0], load.at[t])
        for t in range(PARTS)
    ]
    for copy in tok_loads:
        copy.start()
    cot_loads = [
        pltpu.make_async_copy(
            cot.at[:, pl.ds(c * ring_cols, ring_cols)], zc.at[c, 0], load.at[PARTS + c])
        for c in range(RING)
    ]
    state_loads = [
        pltpu.make_async_copy(
            ref.at[:, pl.ds(c * chunk, chunk)],
            gbuf.at[(a * CHUNKS + c) // NY, (a * CHUNKS + c) % NY],
            load.at[PARTS + RING + a * CHUNKS + c])
        for a, ref in enumerate((weight, moment1, moment2)) for c in range(CHUNKS)
    ]
    for copy in state_loads + cot_loads:
        copy.start()
    top = ids.shape[0]
    zm[0, 0:top] = ids[...].astype(f32)
    zm[0, top:] = gates[...]

    barrier = pltpu.get_barrier_semaphore()

    @pl.loop(1, TOTAL)
    def _(o):
        pl.semaphore_signal(
            barrier, inc=1, device_id=(y, lax.rem(e + o, TOTAL)), device_id_type=MESH)

    for o in range(1, NY):
        pl.semaphore_signal(barrier, inc=1, device_id=layer(o)[1], device_id_type=MESH)
    pl.semaphore_wait(barrier, TOTAL - 1 + NY - 1)

    def remote(src, dst, send, recv, device):
        return pltpu.make_async_remote_copy(
            src_ref=src, dst_ref=dst, send_sem=send, recv_sem=recv,
            device_id=device, device_id_type=MESH,
        )

    def held(direction, step):
        return 0 if step == 1 else 2 * (step - 1) + direction

    def landing(direction, step):
        return 1 if step == 4 else 2 * step + direction

    half = TOK // 2

    def z_copy(ring, send, recv, direction, step):
        src, dst = ring.at[held(direction, step)], ring.at[landing(direction, step)]
        if step == 4:
            rows = pl.ds(direction * half, half)
            src, dst = src.at[rows], dst.at[rows]
        return remote(src, dst, send.at[direction, step], recv.at[direction, step],
                      left if direction else right)

    def tok_copy(t, direction, step):
        return z_copy(zt.at[t], zt_s.at[t], zt_r.at[t], direction, step)

    def cot_copy(c, direction, step):
        return z_copy(zc.at[c], zc_s.at[c], zc_r.at[c], direction, step)

    def meta_copy(direction, step):
        return remote(zm.at[held(direction, step)], zm.at[landing(direction, step)],
                      zm_s.at[direction, step], zm_r.at[direction, step],
                      left if direction else right)

    def meta_steps(step):
        return (0,) if step == 4 else (0, 1)

    for d in (0, 1):
        meta_copy(d, 1).start()
    for t in range(PARTS):
        tok_loads[t].wait()
        for d in (0, 1):
            tok_copy(t, d, 1).start()

    def piece_of(q):
        rows = pl.ds(pl.multiple_of((q // ACROSS) * HIGH, HIGH), HIGH)
        cols = pl.ds(pl.multiple_of(lax.rem(q, ACROSS) * LANES, LANES), LANES)
        return rows, cols

    def all_pieces(buffer, index):
        span = pl.ds(0, TOTAL - 1)
        return remote(buffer.at[span], buffer.at[span], ex_s.at[index], ex_r.at[index], right)

    @pl.loop(1, TOTAL)
    def _(o):
        q = lax.rem(e + o, TOTAL)
        rows, cols = piece_of(q)
        remote(up.at[rows, cols], upmid.at[e], ex_s.at[0], ex_r.at[0], (y, q)).start()

    own_rows, own_cols = piece_of(e)
    own_up = pltpu.make_async_copy(up.at[own_rows, own_cols], upmid.at[e], loc.at[0])
    own_up.start()

    for copy in state_loads:
        copy.wait()

    @pl.loop(0, CHUNKS)
    def _(c):
        for h in range(per_chunk):
            for g in range(groups):
                q = g * ACROSS + c * per_chunk + h
                powers = jnp.zeros((1, LANES), i32)
                for a in range(STATES):
                    x = gbuf[(a * CHUNKS + c) // NY, lax.rem(a * CHUNKS + c, NY), g * HIGH:(g + 1) * HIGH, h * LANES:(h + 1) * LANES]
                    most = jnp.maximum(jnp.max(jnp.abs(x), axis=0, keepdims=True), SMALLEST)
                    power = jnp.ceil(jnp.log(most) * (1.0 / STEP))
                    inverse = 1.0 / (jnp.exp(power * STEP) * (1.0 / LEVELS))
                    code = jnp.clip(jnp.floor(x * inverse + 0.5), -LEVELS, LEVELS).astype(i32)
                    stg[q, a * WORDS:(a + 1) * WORDS] = code[:WORDS] * 65536 + (code[WORDS:] + 32768)
                    powers = powers + (power.astype(i32) + 512) * 1024 ** a
                stg[q, STATES * WORDS:] = powers

    def up_copy(o):
        k, device = layer(o)
        return remote(upb.at[y], upb.at[y], up_s.at[o], up_r.at[o], device)

    row_of = lax.broadcasted_iota(i32, (TOK, TOK), 0)
    col_of = lax.broadcasted_iota(i32, (TOK, TOK), 1)
    before = (row_of < col_of).astype(f32).astype(bf16)
    place_of = lax.broadcasted_iota(i32, (PLANE, CAP, TOK), 1).astype(f32)
    which = lax.broadcasted_iota(i32, (PLANE, TOK), 0)
    expert_of = jnp.zeros((PLANE, TOK), i32)
    for k in range(PLANE):
        expert_of = jnp.where(which == k, match[z * PLANE + k], expert_of)
    expert_of = expert_of.astype(f32)

    def select_of(slot):
        mask = jnp.zeros((PLANE, TOK), f32)
        weights = jnp.zeros((PLANE, TOK), f32)
        for k in range(top):
            hit = zm[slot, k:k + 1, :] == expert_of
            mask = jnp.where(hit, 1.0, mask)
            weights = jnp.where(hit, zm[slot, top + k:top + k + 1, :], weights)
        rank = jnp.dot(mask.astype(bf16), before, preferred_element_type=f32)
        rank = jnp.where(mask > 0.5, rank, -1.0)
        picked = jnp.where(rank[:, None, :] == place_of, 1.0, 0.0)
        gate = jnp.sum(picked * weights[:, None, :], axis=2, keepdims=True)
        return picked, gate

    def build(j):
        first_pick, first_gate = select_of(2 * j)
        second_pick, second_gate = select_of(2 * j + 1)
        blank = jnp.zeros((PLANE, CAP, TOK), f32)
        both = jnp.concatenate(
            [jnp.concatenate([first_pick, blank], axis=2),
             jnp.concatenate([blank, second_pick], axis=2)], axis=1)
        sel[j] = both.reshape(PLANE * 2 * CAP, 2 * TOK).astype(bf16)
        prob[j] = jnp.concatenate([first_gate, second_gate], axis=1).reshape(PLANE * 2 * CAP, 1)

    def xt_copy(j, t, o):
        q, device = mate(o)
        cols = pl.ds(t * part, part)
        return remote(sbt.at[j, q, :, cols], rbt.at[p, j, :, cols],
                      xt_s.at[j, t, o], xt_r.at[j, t, o], device)

    def xt_own(j):
        return pltpu.make_async_copy(sbt.at[j, p], rbt.at[p, j], loc.at[1 + j])

    def xc_copy(c, o):
        q, device = mate(o)
        return remote(sbs.at[c, q], rbs.at[c, p], xc_s.at[c, o], xc_r.at[c, o], device)

    def xc_own(c):
        return pltpu.make_async_copy(sbs.at[c, p], rbs.at[c, p], loc.at[1 + PAIRS + c])

    order = (4, 2, 6, 3, 5, 1, 7)

    def send_tokens(j, t):
        @pl.loop(0, part // 512)
        def _(c):
            cols = pl.ds(pl.multiple_of(c * 512, 512), 512)
            pair = zt[t, 2 * j:2 * j + 2, :, cols].reshape(2 * TOK, 512)
            rows = jnp.dot(sel[j], pair, preferred_element_type=f32)
            there = pl.ds(pl.multiple_of(t * part + c * 512, 512), 512)
            sbt[j, :, :, there] = rows.astype(bf16).reshape(PLANE, 2 * CAP, 512)

        for o in order:
            xt_copy(j, t, o).start()

    landed = upb.at[y, own_rows, own_cols]
    last_up = pltpu.make_async_copy(upout.at[e], landed, loc.at[1 + PAIRS + CHUNKS])

    for step in (1, 2, 3, 4):
        for d in (0, 1):
            if d in meta_steps(step):
                meta_copy(d, step).wait_recv()
                if step < 4 and d in meta_steps(step + 1):
                    meta_copy(d, step + 1).start()
        j = 0 if step == 4 else step
        for t in range(PARTS):
            for d in (0, 1):
                tok_copy(t, d, step).wait_recv()
                if step < 4:
                    tok_copy(t, d, step + 1).start()
            if t == 0:
                build(j)
            send_tokens(j, t)
        xt_own(j).start()
        if step == 2:
            for c in range(RING):
                cot_loads[c].wait()
                for d in (0, 1):
                    cot_copy(c, d, 1).start()
        if step == 2:
            own_up.wait()
            all_pieces(upmid, 0).wait_recv()

            @pl.loop(0, TOTAL)
            def _(i):
                upout[i] = upmid[match[i]]

            @pl.loop(1, TOTAL)
            def _(o):
                q = lax.rem(e + o, TOTAL)
                remote(upout.at[q], landed, ex_s.at[2], ex_r.at[2], (y, q)).start()

            last_up.start()

    last_up.wait()
    all_pieces(upout, 2).wait_recv()
    for o in (2, 1, 3):
        up_copy(o).start()

    for step in (1, 2, 3, 4):
        for r in range(RING):
            for d in (0, 1):
                cot_copy(r, d, step).wait_recv()
                if step < 4:
                    cot_copy(r, d, step + 1).start()
            ratio = CHUNKS // RING
            for c in range(r * ratio, (r + 1) * ratio) if step == 4 else ():
                across = slice((c % ratio) * chunk, (c % ratio + 1) * chunk)
                for j in range(PAIRS):
                    pair = zc[r, 2 * j:2 * j + 2, :, across].reshape(2 * TOK, chunk)
                    rows = jnp.dot(sel[j], pair, preferred_element_type=f32) * prob[j]
                    sbs[c, :, j] = rows.astype(bf16).reshape(PLANE, 2 * CAP, chunk)
                xc_own(c).start()
                for o in order:
                    xc_copy(c, o).start()
        if step == SPREAD_AFTER:
            @pl.loop(1, TOTAL)
            def _(o):
                q = lax.rem(e + o, TOTAL)
                remote(stg.at[q], mid.at[e], ex_s.at[1], ex_r.at[1], (y, q)).start()

            mid[e] = stg[e]

    for o in range(1, NY):
        up_copy(o).wait_recv()
    for j in range(PAIRS):
        xt_own(j).wait()
        for o in range(1, PLANE):
            for t in range(PARTS):
                xt_copy(j, t, o).wait_recv()
    span = 2 * PAIRS * 2 * CAP

    @pl.loop(0, PLANE // 2)
    def _(m):
        rows = rbt[pl.ds(2 * m, 2)].reshape(span, width)
        cols = pl.ds(pl.multiple_of(m * span, span), span)

        @pl.loop(0, NY)
        def _(k):
            v = lax.dot_general(upb[k], rows, (((1,), (1,)), ((), ())), preferred_element_type=f32)
            units = pl.ds(pl.multiple_of(k * slice_rows, slice_rows), slice_rows)
            hid[units, cols] = (v / (1.0 + jnp.exp(-v))).astype(bf16)

    def g_copy(c, o):
        k, device = layer(o)
        return remote(gbuf.at[c, k], grecv.at[c, o - 1], g_s.at[c, o], g_r.at[c, o], device)

    for c in range(CHUNKS):
        xc_own(c).wait()
        for o in range(1, PLANE):
            xc_copy(c, o).wait_recv()

        @pl.loop(0, NY)
        def _(k):
            units = pl.ds(pl.multiple_of(k * slice_rows, slice_rows), slice_rows)
            rows = rbs[c].reshape(PLANE * PAIRS * 2 * CAP, chunk)
            gbuf[c, k] = jnp.dot(hid[units, :], rows, preferred_element_type=f32)

        for o in (2, 1, 3):
            g_copy(c, o).start()
        if c == GATHER_AFTER:
            all_pieces(stg, 1).wait_send()
            all_pieces(mid, 1).wait_recv()

            @pl.loop(0, TOTAL)
            def _(i):
                stg[i] = mid[match[i]]

            @pl.loop(1, TOTAL)
            def _(o):
                q = lax.rem(e + o, TOTAL)
                remote(stg.at[q], fin.at[e], ex_s.at[3], ex_r.at[3], (y, q)).start()

            fin[e] = stg[e]

    all_pieces(fin, 3).wait_recv()
    norm[...] = jnp.zeros_like(norm)

    def put(ref, c, slot):
        return pltpu.make_async_copy(
            gbuf.at[c, slot], ref.at[:, pl.ds(c * chunk, chunk)], store.at[c, slot])

    for c in range(CHUNKS):
        for o in range(1, NY):
            g_copy(c, o).wait()

        @pl.loop(0, groups)
        def _(g):
            rows = pl.ds(pl.multiple_of(g * HIGH, HIGH), HIGH)
            for h in range(per_chunk):
                q = g * ACROSS + c * per_chunk + h
                cols = slice(h * LANES, (h + 1) * LANES)
                powers = fin[q, STATES * WORDS:]

                def state(a):
                    word = fin[q, a * WORDS:(a + 1) * WORDS]
                    upper = lax.shift_right_arithmetic(word, jnp.int32(16))
                    lower = lax.bitwise_and(word, jnp.int32(65535)) - 32768
                    field = lax.shift_right_arithmetic(powers, jnp.int32(10 * a))
                    power = (lax.bitwise_and(field, jnp.int32(1023)) - 512).astype(f32)
                    scale = jnp.exp(power * STEP) * (1.0 / LEVELS)
                    return jnp.concatenate([upper, lower], axis=0).astype(f32) * scale

                gradient = (gbuf[c, y, rows, cols] + grecv[c, 0, rows, cols]) + (
                    grecv[c, 1, rows, cols] + grecv[c, 2, rows, cols])
                old = state(0)
                first = beta_one * state(1) + (1.0 - beta_one) * gradient
                second = beta_two * state(2) + (1.0 - beta_two) * gradient * gradient
                update = first / (jnp.sqrt(second) + epsilon)
                gbuf[c, 0, rows, cols] = first
                gbuf[c, 1, rows, cols] = second
                gbuf[c, 2, rows, cols] = update
                gbuf[c, 3, rows, cols] = old
                norm[0:8] += jnp.sum((old * old).reshape(HIGH // 8, 8, LANES), axis=0)
                norm[8:16] += jnp.sum((update * update).reshape(HIGH // 8, 8, LANES), axis=0)

        put(new_1, c, 0).start()
        put(new_2, c, 1).start()

    def n_copy(o):
        return remote(norm, norm_in.at[o - 1], n_s.at[o], n_r.at[o], layer(o)[1])

    for o in range(1, NY):
        n_copy(o).start()
    for o in range(1, NY):
        n_copy(o).wait_recv()
    squares = (norm[...] + norm_in[0]) + (norm_in[1] + norm_in[2])
    weight_sq = jnp.sum(jnp.sum(squares[0:8], axis=0, keepdims=True), axis=1, keepdims=True)
    update_sq = jnp.sum(jnp.sum(squares[8:16], axis=0, keepdims=True), axis=1, keepdims=True)
    trust = jnp.sqrt(weight_sq) / (jnp.sqrt(update_sq) + epsilon)
    rate = learn_rate * trust
    for c in range(CHUNKS):
        gbuf[c, 3] = gbuf[c, 3] - rate * gbuf[c, 2]
        put(new_w, c, 3).start()

    for step in (1, 2, 3, 4):
        for d in (0, 1):
            if d in meta_steps(step):
                meta_copy(d, step).wait_send()
            for t in range(PARTS):
                tok_copy(t, d, step).wait_send()
            for c in range(RING):
                cot_copy(c, d, step).wait_send()
    all_pieces(upmid, 0).wait_send()
    all_pieces(upout, 2).wait_send()
    all_pieces(stg, 3).wait_send()
    for o in range(1, NY):
        up_copy(o).wait_send()
        n_copy(o).wait_send()
    for o in range(1, PLANE):
        for j in range(PAIRS):
            for t in range(PARTS):
                xt_copy(j, t, o).wait_send()
        for c in range(CHUNKS):
            xc_copy(c, o).wait_send()
    for c in range(CHUNKS):
        put(new_1, c, 0).wait()
        put(new_2, c, 1).wait()
        put(new_w, c, 3).wait()


def local(
    tokens, cotangent, expert_ids, gate_probs, up_weight, down_weight, moment1, moment2, pair_match
):
    rows, width = tokens.shape
    chunk = width // CHUNKS
    units = up_weight.shape[2]
    bf16, f32 = jnp.bfloat16, jnp.float32
    ids, gates = expert_ids.T, gate_probs.T
    up = up_weight[0].T
    pick = PLANE * 2 * CAP
    words = STATES * WORDS + 1
    dma = pltpu.SemaphoreType.DMA
    anywhere = pl.BlockSpec(memory_space=pl.ANY)
    outs = pl.pallas_call(
        step_kernel,
        out_shape=[jax.ShapeDtypeStruct((units, width), f32)] * 3,
        in_specs=[
            pl.BlockSpec(memory_space=pltpu.SMEM),
            pl.BlockSpec(memory_space=pltpu.VMEM), pl.BlockSpec(memory_space=pltpu.VMEM),
        ] + [anywhere] * 6,
        out_specs=[anywhere] * 3,
        scratch_shapes=[
            pltpu.VMEM((PARTS, NZ, rows, width // PARTS), bf16),
            pltpu.VMEM((RING, NZ, rows, width // RING), bf16),
            pltpu.VMEM((NZ, 2 * ids.shape[0], rows), f32),
            pltpu.VMEM((PAIRS, pick, 2 * rows), bf16),
            pltpu.VMEM((PAIRS, pick, 1), f32),
            pltpu.VMEM((PAIRS, PLANE, 2 * CAP, width), bf16),
            pltpu.VMEM((CHUNKS, PLANE, PAIRS, 2 * CAP, chunk), bf16),
            pltpu.VMEM((PLANE, PAIRS, 2 * CAP, width), bf16),
            pltpu.VMEM((CHUNKS, PLANE, PAIRS, 2 * CAP, chunk), bf16),
            pltpu.VMEM((NY, units, width), bf16),
            pltpu.VMEM((NY * units, PAIRS * pick), bf16),
            pltpu.VMEM((CHUNKS, NY, units, chunk), f32),
            pltpu.VMEM((CHUNKS, NY - 1, units, chunk), f32),
            pltpu.VMEM((TOTAL, words, LANES), jnp.int32),
            pltpu.VMEM((TOTAL, words, LANES), jnp.int32),
            pltpu.VMEM((TOTAL, words, LANES), jnp.int32),
            pltpu.VMEM((TOTAL, HIGH, LANES), bf16),
            pltpu.VMEM((TOTAL, HIGH, LANES), bf16),
            pltpu.VMEM((16, LANES), f32),
            pltpu.VMEM((NY - 1, 16, LANES), f32),
            dma((PARTS, 2, 5)), dma((PARTS, 2, 5)),
            dma((2, 5)), dma((2, 5)),
            dma((RING, 2, 5)), dma((RING, 2, 5)),
            dma((NY,)), dma((NY,)),
            dma((PAIRS, PARTS, PLANE)), dma((PAIRS, PARTS, PLANE)),
            dma((CHUNKS, PLANE)), dma((CHUNKS, PLANE)),
            dma((CHUNKS, NY)), dma((CHUNKS, NY)),
            dma((NY,)), dma((NY,)),
            dma((4,)), dma((4,)),
            dma((2 + PAIRS + CHUNKS,)),
            dma((PARTS + RING + STATES * CHUNKS,)),
            dma((CHUNKS, 4)),
        ],
        compiler_params=pltpu.CompilerParams(
            collective_id=0, has_side_effects=True, vmem_limit_bytes=VMEM_BYTES
        ),
        cost_estimate=pl.CostEstimate(
            flops=4 * PAIRS * pick * width * units * NY,
            bytes_accessed=4 * rows * width + 26 * units * width,
            transcendentals=PAIRS * pick * units * NY,
        ),
    )(pair_match, ids, gates, tokens, cotangent, up, down_weight[0], moment1[0], moment2[0])
    return tuple(out[None] for out in outs)


def solution(mesh):
    in_specs = (
        P(("dp", "expert"), None),
        P(("dp", "expert"), None),
        P(("dp", "expert"), None),
        P(("dp", "expert"), None),
        P("expert", None, "dp"),
        P("expert", "dp", None),
        P("expert", "dp", None),
        P("expert", "dp", None),
        P(),
    )
    out_specs = (P("expert", "dp", None), P("expert", "dp", None), P("expert", "dp", None))
    return jax.shard_map(local, mesh=mesh, in_specs=in_specs, out_specs=out_specs, check_vma=False)
```

```python
import jax
import jax.numpy as jnp
from jax import lax
from jax.experimental import pallas as pl
from jax.experimental.pallas import tpu as pltpu
from jax.sharding import PartitionSpec as P

beta_one = 0.9
beta_two = 0.999
epsilon = 1e-06
learn_rate = 0.05

NZ = 8
PLANE = 8
NY = 4
CAP = 24
TOK = 128
PAIRS = NZ // 2
CHUNKS = 8
RING = 4
PARTS = 2
SPREAD_AFTER = 3
GATHER_AFTER = 4
VMEM_BYTES = 62 * 2**20
TOTAL = NZ * PLANE
HIGH, LANES = 48, 128
ACROSS = 16
WORDS = HIGH // 2
STATES = 3
STEP = 0.6931471805599453 / 8.0
LEVELS = 32767.0
SMALLEST = 2.0**-63
MESH = pl.DeviceIdType.MESH


def step_kernel(
    match, ids, gates, tok, cot, up, weight, moment1, moment2, new_w, new_1, new_2,
    zt, zc, zm, sel, prob, sbt, sbs, rbt, rbs, upb, hid, gbuf, grecv,
    stg, mid, fin, upmid, upout, norm, norm_in,
    zt_s, zt_r, zm_s, zm_r, zc_s, zc_r, up_s, up_r, xt_s, xt_r, xc_s, xc_r, g_s, g_r, n_s, n_r,
    ex_s, ex_r, loc, load, store,
):
    f32, bf16, i32 = jnp.float32, jnp.bfloat16, jnp.int32
    width = tok.shape[1]
    chunk = width // CHUNKS
    per_chunk = chunk // LANES
    ring_cols = width // RING
    part = width // PARTS
    slice_rows = up.shape[0]
    groups = slice_rows // HIGH
    y = lax.axis_index("dp")
    e = lax.axis_index("expert")
    z = e // PLANE
    p = lax.rem(e, PLANE)
    right = (y, lax.rem(e + PLANE, TOTAL))
    left = (y, lax.rem(e + TOTAL - PLANE, TOTAL))

    def mate(o):
        q = lax.rem(p + o, PLANE)
        return q, (y, z * PLANE + q)

    def layer(o):
        k = lax.rem(y + o, NY)
        return k, (k, e)

    tok_loads = [
        pltpu.make_async_copy(tok.at[:, pl.ds(t * part, part)], zt.at[t, 0], load.at[t])
        for t in range(PARTS)
    ]
    for copy in tok_loads:
        copy.start()
    cot_loads = [
        pltpu.make_async_copy(
            cot.at[:, pl.ds(c * ring_cols, ring_cols)], zc.at[c, 0], load.at[PARTS + c])
        for c in range(RING)
    ]
    state_loads = [
        pltpu.make_async_copy(
            ref.at[:, pl.ds(c * chunk, chunk)],
            gbuf.at[(a * CHUNKS + c) // NY, (a * CHUNKS + c) % NY],
            load.at[PARTS + RING + a * CHUNKS + c])
        for a, ref in enumerate((weight, moment1, moment2)) for c in range(CHUNKS)
    ]
    for copy in state_loads + cot_loads:
        copy.start()
    top = ids.shape[0]
    zm[0, 0:top] = ids[...].astype(f32)
    zm[0, top:] = gates[...]

    barrier = pltpu.get_barrier_semaphore()

    @pl.loop(1, TOTAL)
    def _(o):
        pl.semaphore_signal(
            barrier, inc=1, device_id=(y, lax.rem(e + o, TOTAL)), device_id_type=MESH)

    for o in range(1, NY):
        pl.semaphore_signal(barrier, inc=1, device_id=layer(o)[1], device_id_type=MESH)
    pl.semaphore_wait(barrier, TOTAL - 1 + NY - 1)

    def remote(src, dst, send, recv, device):
        return pltpu.make_async_remote_copy(
            src_ref=src, dst_ref=dst, send_sem=send, recv_sem=recv,
            device_id=device, device_id_type=MESH,
        )

    def held(direction, step):
        return 0 if step == 1 else 2 * (step - 1) + direction

    def landing(direction, step):
        return 1 if step == 4 else 2 * step + direction

    half = TOK // 2

    def z_copy(ring, send, recv, direction, step):
        src, dst = ring.at[held(direction, step)], ring.at[landing(direction, step)]
        if step == 4:
            rows = pl.ds(direction * half, half)
            src, dst = src.at[rows], dst.at[rows]
        return remote(src, dst, send.at[direction, step], recv.at[direction, step],
                      left if direction else right)

    def tok_copy(t, direction, step):
        return z_copy(zt.at[t], zt_s.at[t], zt_r.at[t], direction, step)

    def cot_copy(c, direction, step):
        return z_copy(zc.at[c], zc_s.at[c], zc_r.at[c], direction, step)

    def meta_copy(direction, step):
        return remote(zm.at[held(direction, step)], zm.at[landing(direction, step)],
                      zm_s.at[direction, step], zm_r.at[direction, step],
                      left if direction else right)

    def meta_steps(step):
        return (0,) if step == 4 else (0, 1)

    for d in (0, 1):
        meta_copy(d, 1).start()
    for t in range(PARTS):
        tok_loads[t].wait()
        for d in (0, 1):
            tok_copy(t, d, 1).start()

    def piece_of(q):
        rows = pl.ds(pl.multiple_of((q // ACROSS) * HIGH, HIGH), HIGH)
        cols = pl.ds(pl.multiple_of(lax.rem(q, ACROSS) * LANES, LANES), LANES)
        return rows, cols

    def all_pieces(buffer, index):
        span = pl.ds(0, TOTAL - 1)
        return remote(buffer.at[span], buffer.at[span], ex_s.at[index], ex_r.at[index], right)

    @pl.loop(1, TOTAL)
    def _(o):
        q = lax.rem(e + o, TOTAL)
        rows, cols = piece_of(q)
        remote(up.at[rows, cols], upmid.at[e], ex_s.at[0], ex_r.at[0], (y, q)).start()

    own_rows, own_cols = piece_of(e)
    own_up = pltpu.make_async_copy(up.at[own_rows, own_cols], upmid.at[e], loc.at[0])
    own_up.start()

    for copy in state_loads:
        copy.wait()

    @pl.loop(0, CHUNKS)
    def _(c):
        for h in range(per_chunk):
            for g in range(groups):
                q = g * ACROSS + c * per_chunk + h
                powers = jnp.zeros((1, LANES), i32)
                for a in range(STATES):
                    x = gbuf[(a * CHUNKS + c) // NY, lax.rem(a * CHUNKS + c, NY), g * HIGH:(g + 1) * HIGH, h * LANES:(h + 1) * LANES]
                    most = jnp.maximum(jnp.max(jnp.abs(x), axis=0, keepdims=True), SMALLEST)
                    power = jnp.ceil(jnp.log(most) * (1.0 / STEP))
                    inverse = 1.0 / (jnp.exp(power * STEP) * (1.0 / LEVELS))
                    code = jnp.clip(jnp.floor(x * inverse + 0.5), -LEVELS, LEVELS).astype(i32)
                    stg[q, a * WORDS:(a + 1) * WORDS] = code[:WORDS] * 65536 + (code[WORDS:] + 32768)
                    powers = powers + (power.astype(i32) + 512) * 1024 ** a
                stg[q, STATES * WORDS:] = powers

    def up_copy(o):
        k, device = layer(o)
        return remote(upb.at[y], upb.at[y], up_s.at[o], up_r.at[o], device)

    row_of = lax.broadcasted_iota(i32, (TOK, TOK), 0)
    col_of = lax.broadcasted_iota(i32, (TOK, TOK), 1)
    before = (row_of < col_of).astype(f32).astype(bf16)
    place_of = lax.broadcasted_iota(i32, (PLANE, CAP, TOK), 1).astype(f32)
    which = lax.broadcasted_iota(i32, (PLANE, TOK), 0)
    expert_of = jnp.zeros((PLANE, TOK), i32)
    for k in range(PLANE):
        expert_of = jnp.where(which == k, match[z * PLANE + k], expert_of)
    expert_of = expert_of.astype(f32)

    def select_of(slot):
        mask = jnp.zeros((PLANE, TOK), f32)
        weights = jnp.zeros((PLANE, TOK), f32)
        for k in range(top):
            hit = zm[slot, k:k + 1, :] == expert_of
            mask = jnp.where(hit, 1.0, mask)
            weights = jnp.where(hit, zm[slot, top + k:top + k + 1, :], weights)
        rank = jnp.dot(mask.astype(bf16), before, preferred_element_type=f32)
        rank = jnp.where(mask > 0.5, rank, -1.0)
        picked = jnp.where(rank[:, None, :] == place_of, 1.0, 0.0)
        gate = jnp.sum(picked * weights[:, None, :], axis=2, keepdims=True)
        return picked, gate

    def build(j):
        first_pick, first_gate = select_of(2 * j)
        second_pick, second_gate = select_of(2 * j + 1)
        blank = jnp.zeros((PLANE, CAP, TOK), f32)
        both = jnp.concatenate(
            [jnp.concatenate([first_pick, blank], axis=2),
             jnp.concatenate([blank, second_pick], axis=2)], axis=1)
        sel[j] = both.reshape(PLANE * 2 * CAP, 2 * TOK).astype(bf16)
        prob[j] = jnp.concatenate([first_gate, second_gate], axis=1).reshape(PLANE * 2 * CAP, 1)

    def xt_copy(j, t, o):
        q, device = mate(o)
        cols = pl.ds(t * part, part)
        return remote(sbt.at[j, q, :, cols], rbt.at[p, j, :, cols],
                      xt_s.at[j, t, o], xt_r.at[j, t, o], device)

    def xt_own(j):
        return pltpu.make_async_copy(sbt.at[j, p], rbt.at[p, j], loc.at[1 + j])

    def xc_copy(c, o):
        q, device = mate(o)
        return remote(sbs.at[c, q], rbs.at[c, p], xc_s.at[c, o], xc_r.at[c, o], device)

    def xc_own(c):
        return pltpu.make_async_copy(sbs.at[c, p], rbs.at[c, p], loc.at[1 + PAIRS + c])

    order = (4, 2, 6, 3, 5, 1, 7)

    def send_tokens(j, t):
        @pl.loop(0, part // 512)
        def _(c):
            cols = pl.ds(pl.multiple_of(c * 512, 512), 512)
            pair = zt[t, 2 * j:2 * j + 2, :, cols].reshape(2 * TOK, 512)
            rows = jnp.dot(sel[j], pair, preferred_element_type=f32)
            there = pl.ds(pl.multiple_of(t * part + c * 512, 512), 512)
            sbt[j, :, :, there] = rows.astype(bf16).reshape(PLANE, 2 * CAP, 512)

        for o in order:
            xt_copy(j, t, o).start()

    landed = upb.at[y, own_rows, own_cols]
    last_up = pltpu.make_async_copy(upout.at[e], landed, loc.at[1 + PAIRS + CHUNKS])

    for step in (1, 2, 3, 4):
        for d in (0, 1):
            if d in meta_steps(step):
                meta_copy(d, step).wait_recv()
                if step < 4 and d in meta_steps(step + 1):
                    meta_copy(d, step + 1).start()
        j = 0 if step == 4 else step
        for t in range(PARTS):
            for d in (0, 1):
                tok_copy(t, d, step).wait_recv()
                if step < 4:
                    tok_copy(t, d, step + 1).start()
            if t == 0:
                build(j)
            send_tokens(j, t)
        xt_own(j).start()
        if step == 3:
            for c in range(RING):
                cot_loads[c].wait()
                for d in (0, 1):
                    cot_copy(c, d, 1).start()
        if step == 2:
            own_up.wait()
            all_pieces(upmid, 0).wait_recv()

            @pl.loop(0, TOTAL)
            def _(i):
                upout[i] = upmid[match[i]]

            @pl.loop(1, TOTAL)
            def _(o):
                q = lax.rem(e + o, TOTAL)
                remote(upout.at[q], landed, ex_s.at[2], ex_r.at[2], (y, q)).start()

            last_up.start()

    last_up.wait()
    all_pieces(upout, 2).wait_recv()
    for o in (2, 1, 3):
        up_copy(o).start()

    for step in (1, 2, 3, 4):
        for r in range(RING):
            for d in (0, 1):
                cot_copy(r, d, step).wait_recv()
                if step < 4:
                    cot_copy(r, d, step + 1).start()
            ratio = CHUNKS // RING
            for c in range(r * ratio, (r + 1) * ratio) if step == 4 else ():
                across = slice((c % ratio) * chunk, (c % ratio + 1) * chunk)
                for j in range(PAIRS):
                    pair = zc[r, 2 * j:2 * j + 2, :, across].reshape(2 * TOK, chunk)
                    rows = jnp.dot(sel[j], pair, preferred_element_type=f32) * prob[j]
                    sbs[c, :, j] = rows.astype(bf16).reshape(PLANE, 2 * CAP, chunk)
                xc_own(c).start()
                for o in order:
                    xc_copy(c, o).start()
        if step == SPREAD_AFTER:
            @pl.loop(1, TOTAL)
            def _(o):
                q = lax.rem(e + o, TOTAL)
                remote(stg.at[q], mid.at[e], ex_s.at[1], ex_r.at[1], (y, q)).start()

            mid[e] = stg[e]

    for o in range(1, NY):
        up_copy(o).wait_recv()
    for j in range(PAIRS):
        xt_own(j).wait()
        for o in range(1, PLANE):
            for t in range(PARTS):
                xt_copy(j, t, o).wait_recv()
    span = 2 * PAIRS * 2 * CAP

    @pl.loop(0, PLANE // 2)
    def _(m):
        rows = rbt[pl.ds(2 * m, 2)].reshape(span, width)
        cols = pl.ds(pl.multiple_of(m * span, span), span)

        @pl.loop(0, NY)
        def _(k):
            v = lax.dot_general(upb[k], rows, (((1,), (1,)), ((), ())), preferred_element_type=f32)
            units = pl.ds(pl.multiple_of(k * slice_rows, slice_rows), slice_rows)
            hid[units, cols] = (v / (1.0 + jnp.exp(-v))).astype(bf16)

    def g_copy(c, o):
        k, device = layer(o)
        return remote(gbuf.at[c, k], grecv.at[c, o - 1], g_s.at[c, o], g_r.at[c, o], device)

    for c in range(CHUNKS):
        xc_own(c).wait()
        for o in range(1, PLANE):
            xc_copy(c, o).wait_recv()

        @pl.loop(0, NY)
        def _(k):
            units = pl.ds(pl.multiple_of(k * slice_rows, slice_rows), slice_rows)
            rows = rbs[c].reshape(PLANE * PAIRS * 2 * CAP, chunk)
            gbuf[c, k] = jnp.dot(hid[units, :], rows, preferred_element_type=f32)

        for o in (2, 1, 3):
            g_copy(c, o).start()
        if c == GATHER_AFTER:
            all_pieces(stg, 1).wait_send()
            all_pieces(mid, 1).wait_recv()

            @pl.loop(0, TOTAL)
            def _(i):
                stg[i] = mid[match[i]]

            @pl.loop(1, TOTAL)
            def _(o):
                q = lax.rem(e + o, TOTAL)
                remote(stg.at[q], fin.at[e], ex_s.at[3], ex_r.at[3], (y, q)).start()

            fin[e] = stg[e]

    all_pieces(fin, 3).wait_recv()
    norm[...] = jnp.zeros_like(norm)

    def put(ref, c, slot):
        return pltpu.make_async_copy(
            gbuf.at[c, slot], ref.at[:, pl.ds(c * chunk, chunk)], store.at[c, slot])

    for c in range(CHUNKS):
        for o in range(1, NY):
            g_copy(c, o).wait()

        @pl.loop(0, groups)
        def _(g):
            rows = pl.ds(pl.multiple_of(g * HIGH, HIGH), HIGH)
            for h in range(per_chunk):
                q = g * ACROSS + c * per_chunk + h
                cols = slice(h * LANES, (h + 1) * LANES)
                powers = fin[q, STATES * WORDS:]

                def state(a):
                    word = fin[q, a * WORDS:(a + 1) * WORDS]
                    upper = lax.shift_right_arithmetic(word, jnp.int32(16))
                    lower = lax.bitwise_and(word, jnp.int32(65535)) - 32768
                    field = lax.shift_right_arithmetic(powers, jnp.int32(10 * a))
                    power = (lax.bitwise_and(field, jnp.int32(1023)) - 512).astype(f32)
                    scale = jnp.exp(power * STEP) * (1.0 / LEVELS)
                    return jnp.concatenate([upper, lower], axis=0).astype(f32) * scale

                gradient = (gbuf[c, y, rows, cols] + grecv[c, 0, rows, cols]) + (
                    grecv[c, 1, rows, cols] + grecv[c, 2, rows, cols])
                old = state(0)
                first = beta_one * state(1) + (1.0 - beta_one) * gradient
                second = beta_two * state(2) + (1.0 - beta_two) * gradient * gradient
                update = first / (jnp.sqrt(second) + epsilon)
                gbuf[c, 0, rows, cols] = first
                gbuf[c, 1, rows, cols] = second
                gbuf[c, 2, rows, cols] = update
                gbuf[c, 3, rows, cols] = old
                norm[0:8] += jnp.sum((old * old).reshape(HIGH // 8, 8, LANES), axis=0)
                norm[8:16] += jnp.sum((update * update).reshape(HIGH // 8, 8, LANES), axis=0)

        put(new_1, c, 0).start()
        put(new_2, c, 1).start()

    def n_copy(o):
        return remote(norm, norm_in.at[o - 1], n_s.at[o], n_r.at[o], layer(o)[1])

    for o in range(1, NY):
        n_copy(o).start()
    for o in range(1, NY):
        n_copy(o).wait_recv()
    squares = (norm[...] + norm_in[0]) + (norm_in[1] + norm_in[2])
    weight_sq = jnp.sum(jnp.sum(squares[0:8], axis=0, keepdims=True), axis=1, keepdims=True)
    update_sq = jnp.sum(jnp.sum(squares[8:16], axis=0, keepdims=True), axis=1, keepdims=True)
    trust = jnp.sqrt(weight_sq) / (jnp.sqrt(update_sq) + epsilon)
    rate = learn_rate * trust
    for c in range(CHUNKS):
        gbuf[c, 3] = gbuf[c, 3] - rate * gbuf[c, 2]
        put(new_w, c, 3).start()

    for step in (1, 2, 3, 4):
        for d in (0, 1):
            if d in meta_steps(step):
                meta_copy(d, step).wait_send()
            for t in range(PARTS):
                tok_copy(t, d, step).wait_send()
            for c in range(RING):
                cot_copy(c, d, step).wait_send()
    all_pieces(upmid, 0).wait_send()
    all_pieces(upout, 2).wait_send()
    all_pieces(stg, 3).wait_send()
    for o in range(1, NY):
        up_copy(o).wait_send()
        n_copy(o).wait_send()
    for o in range(1, PLANE):
        for j in range(PAIRS):
            for t in range(PARTS):
                xt_copy(j, t, o).wait_send()
        for c in range(CHUNKS):
            xc_copy(c, o).wait_send()
    for c in range(CHUNKS):
        put(new_1, c, 0).wait()
        put(new_2, c, 1).wait()
        put(new_w, c, 3).wait()


def local(
    tokens, cotangent, expert_ids, gate_probs, up_weight, down_weight, moment1, moment2, pair_match
):
    rows, width = tokens.shape
    chunk = width // CHUNKS
    units = up_weight.shape[2]
    bf16, f32 = jnp.bfloat16, jnp.float32
    ids, gates = expert_ids.T, gate_probs.T
    up = up_weight[0].T
    pick = PLANE * 2 * CAP
    words = STATES * WORDS + 1
    dma = pltpu.SemaphoreType.DMA
    anywhere = pl.BlockSpec(memory_space=pl.ANY)
    outs = pl.pallas_call(
        step_kernel,
        out_shape=[jax.ShapeDtypeStruct((units, width), f32)] * 3,
        in_specs=[
            pl.BlockSpec(memory_space=pltpu.SMEM),
            pl.BlockSpec(memory_space=pltpu.VMEM), pl.BlockSpec(memory_space=pltpu.VMEM),
        ] + [anywhere] * 6,
        out_specs=[anywhere] * 3,
        scratch_shapes=[
            pltpu.VMEM((PARTS, NZ, rows, width // PARTS), bf16),
            pltpu.VMEM((RING, NZ, rows, width // RING), bf16),
            pltpu.VMEM((NZ, 2 * ids.shape[0], rows), f32),
            pltpu.VMEM((PAIRS, pick, 2 * rows), bf16),
            pltpu.VMEM((PAIRS, pick, 1), f32),
            pltpu.VMEM((PAIRS, PLANE, 2 * CAP, width), bf16),
            pltpu.VMEM((CHUNKS, PLANE, PAIRS, 2 * CAP, chunk), bf16),
            pltpu.VMEM((PLANE, PAIRS, 2 * CAP, width), bf16),
            pltpu.VMEM((CHUNKS, PLANE, PAIRS, 2 * CAP, chunk), bf16),
            pltpu.VMEM((NY, units, width), bf16),
            pltpu.VMEM((NY * units, PAIRS * pick), bf16),
            pltpu.VMEM((CHUNKS, NY, units, chunk), f32),
            pltpu.VMEM((CHUNKS, NY - 1, units, chunk), f32),
            pltpu.VMEM((TOTAL, words, LANES), jnp.int32),
            pltpu.VMEM((TOTAL, words, LANES), jnp.int32),
            pltpu.VMEM((TOTAL, words, LANES), jnp.int32),
            pltpu.VMEM((TOTAL, HIGH, LANES), bf16),
            pltpu.VMEM((TOTAL, HIGH, LANES), bf16),
            pltpu.VMEM((16, LANES), f32),
            pltpu.VMEM((NY - 1, 16, LANES), f32),
            dma((PARTS, 2, 5)), dma((PARTS, 2, 5)),
            dma((2, 5)), dma((2, 5)),
            dma((RING, 2, 5)), dma((RING, 2, 5)),
            dma((NY,)), dma((NY,)),
            dma((PAIRS, PARTS, PLANE)), dma((PAIRS, PARTS, PLANE)),
            dma((CHUNKS, PLANE)), dma((CHUNKS, PLANE)),
            dma((CHUNKS, NY)), dma((CHUNKS, NY)),
            dma((NY,)), dma((NY,)),
            dma((4,)), dma((4,)),
            dma((2 + PAIRS + CHUNKS,)),
            dma((PARTS + RING + STATES * CHUNKS,)),
            dma((CHUNKS, 4)),
        ],
        compiler_params=pltpu.CompilerParams(
            collective_id=0, has_side_effects=True, vmem_limit_bytes=VMEM_BYTES
        ),
        cost_estimate=pl.CostEstimate(
            flops=4 * PAIRS * pick * width * units * NY,
            bytes_accessed=4 * rows * width + 26 * units * width,
            transcendentals=PAIRS * pick * units * NY,
        ),
    )(pair_match, ids, gates, tokens, cotangent, up, down_weight[0], moment1[0], moment2[0])
    return tuple(out[None] for out in outs)


def solution(mesh):
    in_specs = (
        P(("dp", "expert"), None),
        P(("dp", "expert"), None),
        P(("dp", "expert"), None),
        P(("dp", "expert"), None),
        P("expert", None, "dp"),
        P("expert", "dp", None),
        P("expert", "dp", None),
        P("expert", "dp", None),
        P(),
    )
    out_specs = (P("expert", "dp", None), P("expert", "dp", None), P("expert", "dp", None))
    return jax.shard_map(local, mesh=mesh, in_specs=in_specs, out_specs=out_specs, check_vma=False)
```
